512 devices in a mesh: freq: 64 (over y, z_hi, x), bl: 8 (over z_lo, core).
Axes of the slice: x: 4, y: 8, z: 8 (z_hi: 2, z_lo: 4; z = z_hi * 4 + z_lo), core: 2. Of those that a mesh axis runs over, the one named last changes fastest.
Arguments:
- visibility_noise: float32 [128, 16, 2, 1024], P('freq', None, None, 'bl'), may hold values from -6 to 6
- baseline_wavelength_coords: float32 [3, 16, 1024], P(None, None, 'bl'), may hold values from -256 to 256
- station_pair: int32 [2, 1024], P(None, 'bl'), may hold values from 0 to 511, as said below
- comp_position: float32 [16, 2, 64], P('bl'), may hold values from -0.1 to 0.1
- comp_flux: float32 [16, 64], P('bl'), may hold values from 0.05 to 1
- comp_spectral: float32 [16, 64], P('bl'), may hold values from -1.5 to 0.5
- comp_count: int32 [16], P('bl'), may hold values from 1 to 64, 512 in all
- true_gains: float32 [128, 16, 2, 512], P('freq'), may hold values from 0.1 to 1.9
- start_gains: float32 [128, 16, 2, 512], P('freq'), may hold values from 0.1 to 1.9
- channel_flags: int32 [128], P('freq'), may hold values 0 or 1
Outputs:
- calibrated_gains: float32 [128, 16, 2, 512], P('freq')
- residual: float32 [128, 16, 2, 1024], P('freq', None, None, 'bl')
The draws below stay inside these ranges and needn't reach their ends.
Inputs may be any that keep to these rules, and one draw needn't show every extreme that they name: `station_pair`: the two stations of a baseline differ. The first comp_count[d] slots of comp_position, comp_flux and comp_spectral of patch d are its components; the later slots are unused.
All inputs are finite; a program needn't handle non-finite values. No bound on the sum of `comp_count` or of `channel_flags` on one device may be relied on, other than what follows from the above.
Results may differ from the reference program's by a relative error of at most 0.0003.
Values sent between devices are 32-bit elements; how exact they have to be, the bound alone decides.
A program may use at most 64 MiB of HBM per device.

```python
import math
import jax
import jax.numpy as jnp
import numpy as np
from jax import lax

STATION_TOTAL = 512
DIRS = 16
REACH = 4
ITERS = 3
CH_DEV = 2
TIMESTEP_TOTAL = 16
CAP = 64
CHANNEL_TOTAL = 128
BASELINE_TOTAL = 1024


def draw_station_pair(key, part):
    key = jax.random.fold_in(key, 11)
    leading_key, offset_random_key = jax.random.split(key)
    leading_station = jax.random.randint(leading_key, (BASELINE_TOTAL,), 0, STATION_TOTAL)
    shift_amounts = jax.random.randint(offset_random_key, (BASELINE_TOTAL,), 1, STATION_TOTAL)
    slot_indices = jnp.arange(BASELINE_TOTAL)
    leading_station = jnp.where(slot_indices == 0, STATION_TOTAL - 1, leading_station)
    shift_amounts = jnp.where(slot_indices == 0, 1, shift_amounts)
    second_station = (leading_station + shift_amounts) % STATION_TOTAL
    return jnp.stack([leading_station, second_station]).astype(jnp.int32)


def place_ends(array, stream_key, least, top_value):
    spot = [jax.random.randint(jax.random.fold_in(stream_key, axis), (), 0, length) for axis, length in enumerate(array.shape)]
    main_axis = array.shape.index(max(array.shape))
    next_to = spot[:main_axis] + [(spot[main_axis] + 1) % array.shape[main_axis]] + spot[main_axis + 1:]
    return array.at[tuple(spot)].set(least).at[tuple(next_to)].set(top_value)


def shard_levels(stream_key, extent, cuts, low, high):
    def one(dim, parts):
        draws = jax.random.uniform(jax.random.fold_in(jax.random.fold_in(stream_key, 6), dim), (parts,), jnp.float32, low / len(cuts), high / len(cuts))
        return jnp.repeat(jnp.exp(draws), extent[dim] // parts).reshape((-1,) + (1,) * (len(extent) - dim - 1))

    loudness = one(*cuts[0])
    for cut in cuts[1:]:
        loudness = loudness * one(*cut)
    return loudness


def length_profile(count, total, bound, lean):
    loads = [(1 << 20) // math.isqrt(rank ** lean) + 1 for rank in range(2, count + 1)]
    rest, counts = total - bound - (count - 1), [1] * (count - 1)
    while rest > 0:
        free = [i for i in range(count - 1) if counts[i] < bound]
        mass, left = sum([loads[i] for i in free]), rest
        for i in free:
            more = min(bound - counts[i], max(1, left * loads[i] // mass), rest)
            counts[i] = counts[i] + more
            rest = rest - more
    return np.array([bound] + counts)


def uneven(rng, amount, total, most, lean):
    if amount == 2:
        one = jax.random.randint(rng, (), max(1, total - most), min(most, total - 1) + 1)
        return jnp.stack([one, total - one])
    lengths = jnp.asarray(length_profile(amount, total, most, lean), jnp.int32)
    pairs = (amount - 1) // 2
    giver, taker = lengths[1:1 + 2 * pairs:2], lengths[2:2 + 2 * pairs:2]
    margin = jnp.minimum(giver - 1, most - taker)
    moved = jax.random.randint(jax.random.fold_in(rng, 1), (pairs,), 0, 1 << 20) % (margin + 1)
    lengths = lengths.at[1:1 + 2 * pairs:2].set(giver - moved).at[2:2 + 2 * pairs:2].set(taker + moved)
    return lengths[jax.random.permutation(jax.random.fold_in(rng, 2), amount)]


def noise(key, shape, scale, bound, shards=(), kind=jnp.bfloat16):
    array = scale * jax.random.normal(key, shape, jnp.float32)
    if shards:
        array = array * shard_levels(key, shape, shards, -0.22, 0.18)
    return jnp.clip(array, -bound, bound).astype(kind)


def setup_inputs(seed: int = 0) -> dict:
    seeds = jax.random.split(jax.random.key(seed), 11)
    return {
        "visibility_noise": noise(seeds[0], (CHANNEL_TOTAL, TIMESTEP_TOTAL, 2, BASELINE_TOTAL), 1.0, 6.0, ((0, 64), (3, 8)), jnp.float32),
        "baseline_wavelength_coords": noise(seeds[1], (3, TIMESTEP_TOTAL, BASELINE_TOTAL), 40.0, 256.0, ((2, 8),), jnp.float32),
        "station_pair": draw_station_pair(jax.random.fold_in(seeds[10], 71), 0),
        "comp_position": jnp.clip(jax.random.uniform(seeds[3], (DIRS, 2, CAP), jnp.float32, -0.1, 0.1) * shard_levels(seeds[3], (DIRS, 2, CAP), ((0, 8),), -0.4, 0.0), -0.1, 0.1),
        "comp_flux": jnp.clip(jnp.exp(math.log(1.0) - 2.9957323 * jax.random.uniform(seeds[4], (DIRS, CAP), jnp.float32) ** shard_levels(seeds[4], (DIRS, CAP), ((0, 8),), -0.2, 0.2)), 0.05, 1.0),
        "comp_spectral": jnp.clip(-1.5 + 2.0 * jax.random.uniform(seeds[5], (DIRS, CAP), jnp.float32) ** shard_levels(seeds[5], (DIRS, CAP), ((0, 8),), -0.2, 0.2), -1.5, 0.5),
        "comp_count": uneven(seeds[6], DIRS, DIRS * CAP // 2, CAP, 2).astype(jnp.int32),
        "true_gains": jnp.clip(1.0 + 0.18 * jax.random.normal(seeds[7], (CHANNEL_TOTAL, DIRS, 2, STATION_TOTAL), jnp.float32), 0.1, 1.9),
        "start_gains": jnp.clip(1.0 + 0.18 * jax.random.normal(seeds[8], (CHANNEL_TOTAL, DIRS, 2, STATION_TOTAL), jnp.float32), 0.1, 1.9),
        "channel_flags": place_ends((jax.random.randint(seeds[9], (CHANNEL_TOTAL,), 0, 4) < 1).astype(jnp.int32), jax.random.fold_in(seeds[9], 1), 0, 1),
    }


TWO_PI = 6.283185307179586

def channel_ratio(first_channel, channel_count, band_total):
    channel_ids = (first_channel + jnp.arange(channel_count)).astype(jnp.float32)
    return 0.5 + (channel_ids + 0.5) / band_total

def patch_model(position, fluxes, spectral, count_one, coords, ratios):
    eastward = position[0]
    northward = position[1]
    depth_term = jnp.sqrt(1.0 - eastward * eastward - northward * northward) - 1.0
    live_mask = (jnp.arange(fluxes.shape[0]) < count_one).astype(jnp.float32)
    spectrum = (fluxes * live_mask)[None, :] * jnp.exp(spectral[None, :] * jnp.log(ratios)[:, None])
    delays = coords[0][None] * eastward[:, None, None] + coords[1][None] * northward[:, None, None] + coords[2][None] * depth_term[:, None, None]

    def one_channel(members):
        scaling, weights = members
        phases = TWO_PI * scaling * delays
        real_part = lax.optimization_barrier(jnp.sum(weights[:, None, None] * jnp.cos(phases), axis=0))
        imag_part = -lax.optimization_barrier(jnp.sum(weights[:, None, None] * jnp.sin(phases), axis=0))
        return jnp.stack([real_part, imag_part], axis=1)
    return lax.map(one_channel, (ratios, spectrum))

def corrupt(gain_now, leading_station, second_station, sky_model):
    gain_first = jnp.take(gain_now, leading_station, axis=2)
    gain_second = jnp.take(gain_now, second_station, axis=2)
    joint_real = gain_first[:, 0] * gain_second[:, 0] + gain_first[:, 1] * gain_second[:, 1]
    joint_imag = gain_first[:, 1] * gain_second[:, 0] - gain_first[:, 0] * gain_second[:, 1]
    model_real = sky_model[:, :, 0]
    model_imag = sky_model[:, :, 1]
    term_real = joint_real[:, None] * model_real - joint_imag[:, None] * model_imag
    term_imag = joint_real[:, None] * model_imag + joint_imag[:, None] * model_real
    return (gain_first, gain_second, term_real, term_imag)

def observe(gain_now, leading_station, second_station, sky_model, noise_part):
    corrupted = corrupt(gain_now, leading_station, second_station, sky_model)
    return jnp.stack([noise_part[:, 0] + lax.optimization_barrier(jnp.sum(corrupted[2], axis=0)), noise_part[:, 1] + lax.optimization_barrier(jnp.sum(corrupted[3], axis=0))], axis=1)

def subtract_sky(gain_now, leading_station, second_station, sky_model, observed):
    corrupted = corrupt(gain_now, leading_station, second_station, sky_model)
    return jnp.stack([observed[:, 0] - lax.optimization_barrier(jnp.sum(corrupted[2], axis=0)), observed[:, 1] - lax.optimization_barrier(jnp.sum(corrupted[3], axis=0))], axis=1)

def station_terms(gain_now, leading_station, second_station, sky_model, observed):
    gain_first, gain_second, term_real, term_imag = corrupt(gain_now, leading_station, second_station, sky_model)
    rest_real = observed[:, 0] - lax.optimization_barrier(jnp.sum(term_real, axis=0))
    rest_imag = observed[:, 1] - lax.optimization_barrier(jnp.sum(term_imag, axis=0))
    single_real = rest_real[None] + term_real
    single_imag = rest_imag[None] + term_imag
    model_real = sky_model[:, :, 0]
    model_imag = sky_model[:, :, 1]
    fitted_real = lax.optimization_barrier(jnp.sum(model_real * single_real + model_imag * single_imag, axis=1))
    fitted_imag = lax.optimization_barrier(jnp.sum(model_real * single_imag - model_imag * single_real, axis=1))
    energy = lax.optimization_barrier(jnp.sum(model_real * model_real + model_imag * model_imag, axis=1))
    first_real = gain_first[:, 0]
    first_imag = gain_first[:, 1]
    second_real = gain_second[:, 0]
    second_imag = gain_second[:, 1]
    toward_first = jnp.stack([second_real * fitted_real - second_imag * fitted_imag, second_real * fitted_imag + second_imag * fitted_real, energy * (second_real * second_real + second_imag * second_imag)], axis=1)
    toward_second = jnp.stack([first_real * fitted_real + first_imag * fitted_imag, first_imag * fitted_real - first_real * fitted_imag, energy * (first_real * first_real + first_imag * first_imag)], axis=1)
    return (toward_first, toward_second)

def update(gain_now, totals, weight):
    scaled = totals * weight[:, None, None, None]
    solved = scaled[:, :, 0:2] / jnp.maximum(scaled[:, :, 2:3], 1.0)
    return 0.5 * gain_now + 0.5 * solved

def kernel(shift_amounts, span):
    distance = shift_amounts.astype(jnp.float32)
    spread = 0.5 * span
    inside = (jnp.abs(shift_amounts) <= span).astype(jnp.float32)
    return jnp.exp(-(distance * distance) / (2.0 * spread * spread)) * inside

def smooth(mixed_gain, weight):
    channel_ids = jnp.arange(CHANNEL_TOTAL).astype(jnp.int32)
    matrix = kernel(channel_ids[:, None] - channel_ids[None, :], REACH * CH_DEV)
    flattened = (weight[:, None, None, None] * mixed_gain).reshape(CHANNEL_TOTAL, -1)
    summed = jnp.dot(matrix, flattened, precision=lax.Precision.HIGHEST).reshape(mixed_gain.shape)
    norm_sums = jnp.dot(matrix, weight, precision=lax.Precision.HIGHEST)
    return summed / jnp.maximum(norm_sums, 1.0)[:, None, None, None]

def reference(visibility_noise, baseline_wavelength_coords, station_pair, comp_position, comp_flux, comp_spectral, comp_count, true_gains, start_gains, channel_flags):
    ratios = channel_ratio(0, CHANNEL_TOTAL, CHANNEL_TOTAL)

    def one_patch(members):
        return patch_model(members[0], members[1], members[2], members[3], baseline_wavelength_coords, ratios)
    patches = lax.map(one_patch, (comp_position, comp_flux, comp_spectral, comp_count))
    sky_model = jnp.transpose(patches, (1, 0, 2, 3, 4))
    leading_station = station_pair[0]
    second_station = station_pair[1]
    weight = 1.0 - channel_flags.astype(jnp.float32)
    observed = lax.map(lambda members: observe(members[0], leading_station, second_station, members[1], members[2]), (true_gains, sky_model, visibility_noise))

    def channel_sums(members):
        toward_first, toward_second = station_terms(members[0], leading_station, second_station, members[1], members[2])
        empty = jnp.zeros((toward_first.shape[0], 3, STATION_TOTAL), jnp.float32)
        return empty.at[:, :, leading_station].add(toward_first).at[:, :, second_station].add(toward_second)
    gain_now = start_gains
    for iteration in range(ITERS):
        totals = lax.map(channel_sums, (gain_now, sky_model, observed))
        gain_now = smooth(update(gain_now, totals, weight), weight)
    residual = lax.map(lambda members: subtract_sky(members[0], leading_station, second_station, members[1], members[2]), (gain_now, sky_model, observed))
    return (gain_now, residual)
```

```python
import jax
import jax.numpy as jnp
from jax import lax
from jax.experimental import pallas as pl
from jax.experimental.pallas import tpu as pltpu
from jax.sharding import PartitionSpec as P

F32 = jnp.float32
BF16 = jnp.bfloat16
MESH = pl.DeviceIdType.MESH
VMEM = pltpu.MemorySpace.VMEM
SMEM = pltpu.MemorySpace.SMEM

BL = 8
LINE = 4
RING = 16
ITERS = 3
DIRS = 16
TIMES = 16
STATIONS = 512
LANES = 128
REACH = 8.0
SPREAD = 4.0

SIN_HALF = (3.1415820213, -5.1671427567, 2.5418986016, -0.5546349618)
COS_HALF = (0.9999932956, -4.9339380202, 4.0412837185, -1.2221263189)


def horner(coefficients, at):
    value = coefficients[-1] * at + coefficients[-2]
    for coefficient in coefficients[-3::-1]:
        value = value * at + coefficient
    return value


def split_two(value):
    high = value.astype(BF16)
    low = (value - high.astype(F32)).astype(BF16)
    return high, low


def ratio_of(channel):
    return 0.5 + (channel.astype(F32) + 0.5) / 128.0


def gather_kernel(position, flux, spectral, count, pair, out, send, recv):
    me = lax.axis_index("bl")
    barrier = pltpu.get_barrier_semaphore()
    for step in range(1, BL):
        pl.semaphore_signal(barrier, inc=1, device_id={"bl": lax.rem(me + step, BL)}, device_id_type=MESH)
    first = lax.axis_index("freq") * 2

    def both(values):
        return jnp.concatenate([values[0:1], values[1:2]], axis=1)

    l = both(position[:, 0, :])
    m = both(position[:, 1, :])
    square = l * l + m * m
    n = -square / (1.0 + jnp.sqrt(1.0 - square))
    fluxes = both(flux[...])
    index = both(spectral[...])
    lane = lax.broadcasted_iota(jnp.int32, (1, LANES), 1)
    out[me, 0:1, :] = l
    out[me, 1:2, :] = m
    out[me, 2:3, :] = n
    extra = jnp.where(lane == 0, count[0].astype(F32), count[1].astype(F32))
    for channel in range(2):
        ratio = jnp.full((1, LANES), 1.0, F32) * ratio_of(first + channel)
        out[me, 3 + channel:4 + channel, :] = fluxes * jnp.exp(index * jnp.log(ratio))
        extra = jnp.where(lane == 2 + channel, ratio, extra)
    out[me, 5:6, :] = extra
    out[me, 6:8, :] = pair[...].astype(F32)

    pl.semaphore_wait(barrier, BL - 1)
    copies = []
    for step in range(1, BL):
        copy = pltpu.make_async_remote_copy(
            src_ref=out.at[me], dst_ref=out.at[me], send_sem=send.at[step], recv_sem=recv.at[step],
            device_id={"bl": lax.rem(me + step, BL)}, device_id_type=MESH)
        copy.start()
        copies.append(copy)
    for copy in copies:
        copy.wait()


def predict_kernel(params, coords, model):
    ratios = [params[5, 2], params[5, 3]]
    unroll = 4

    def one_patch(patch, _):
        row = (patch // 2) * 8
        column = (patch % 2) * 64
        live = params[row + 5, patch % 2].astype(jnp.int32)

        def some(turn, sums):
            sums = list(sums)
            for part in range(unroll):
                slot = turn * unroll + part
                at = column + slot
                l, m, n = params[row, at], params[row + 1, at], params[row + 2, at]
                delay = coords[0] * l + coords[1] * m + coords[2] * n
                for channel in range(2):
                    weight = jnp.where(slot < live, params[row + 3 + channel, at], 0.0)
                    turns = delay * ratios[channel]
                    turns = turns - jnp.round(turns)
                    square = turns * turns
                    sine = turns * horner(SIN_HALF, square)
                    cosine = horner(COS_HALF, square)
                    scaled = sine * weight
                    sums[3 * channel] += scaled * sine
                    sums[3 * channel + 1] += scaled * cosine
                    sums[3 * channel + 2] += weight
            return tuple(sums)

        zero = jnp.zeros((TIMES, LANES), F32)
        sums = lax.fori_loop(0, (live + unroll - 1) // unroll, some, (zero, zero, F32(0.0)) * 2)
        for channel in range(2):
            model[channel, patch, 0] = sums[3 * channel + 2] - 2.0 * sums[3 * channel]
            model[channel, patch, 1] = -2.0 * sums[3 * channel + 1]
        return 0

    lax.fori_loop(0, DIRS, one_patch, 0)


def calibrate_kernel(noise, model, params, true_gains, start_gains, flags,
                     gains_out, residual_out,
                     onehot, observed, joint_true, firsts, seconds, owned, first_out, first_in,
                     energy, energy_in, fits, fits_in, joint_out, joint_in, mixed, stage,
                     s_first, r_first, s_energy, r_energy, s_fit, r_fit, s_joint, r_joint,
                     s_mix, r_mix, s_gain, r_gain):
    freq = lax.axis_index("freq")
    bl = lax.axis_index("bl")
    y = lax.div(freq, 8)
    z_hi = lax.rem(lax.div(freq, LINE), 2)
    x = lax.rem(freq, LINE)
    me = z_hi * BL + bl
    above, below = y < lax.axis_size("freq") // 8 - 1, y > 0

    def ring(step):
        other = lax.rem(me + step, RING)
        device = {"freq": (y * 2 + lax.div(other, BL)) * LINE + x, "bl": lax.rem(other, BL)}
        return other, device

    def plane(other_y, other_x):
        return {"freq": (other_y * 2 + z_hi) * LINE + other_x, "bl": bl}

    mixed[...] = jnp.zeros(mixed.shape, F32)

    barrier = pltpu.get_barrier_semaphore()
    for step in range(1, RING):
        pl.semaphore_signal(barrier, inc=1, device_id=ring(step)[1], device_id_type=MESH)
    for step in range(1, LINE):
        pl.semaphore_signal(barrier, inc=1, device_id=plane(y, lax.rem(x + step, LINE)), device_id_type=MESH)

    @pl.when(above)
    def _():
        for other_x in range(LINE):
            pl.semaphore_signal(barrier, inc=1, device_id=plane(y + 1, other_x), device_id_type=MESH)

    @pl.when(below)
    def _():
        for other_x in range(LINE):
            pl.semaphore_signal(barrier, inc=1, device_id=plane(y - 1, other_x), device_id_type=MESH)

    station = lax.broadcasted_iota(jnp.int32, (STATIONS, LANES), 0).astype(F32)
    for source in range(BL):
        for end in range(2):
            ids = params[source * 8 + 6 + end:source * 8 + 7 + end, :]
            start = (source * 2 + end) * LANES
            onehot[:, start:start + LANES] = jnp.where(station == ids, 1.0, 0.0).astype(BF16)

    def local_joint(gains):
        own_onehot = onehot[:, pl.ds(pl.multiple_of(bl * 2 * LANES, 2 * LANES), 2 * LANES)]
        rows = []
        for part in range(2):
            rows.append(jnp.concatenate(
                [gains[pl.ds(tile * 2 + part, 32, stride=8), :] for tile in range(4)], axis=1))
        high, low = split_two(jnp.concatenate(rows, axis=0))
        ends = jnp.dot(jnp.concatenate([high, low], axis=0), own_onehot, preferred_element_type=F32)
        ends = ends[0:64] + ends[64:128]
        pr, pi = ends[0:32, 0:LANES], ends[32:64, 0:LANES]
        qr, qi = ends[0:32, LANES:], ends[32:64, LANES:]
        return pr * qr + pi * qi, pi * qr - pr * qi

    for ref, gains in ((joint_true, true_gains), (joint_in.at[0], start_gains)):
        parts = local_joint(gains)
        for channel in range(2):
            for part in range(2):
                for patch in range(DIRS):
                    at = channel * DIRS + patch
                    ref[patch, part * 2 + channel:part * 2 + channel + 1, :] = parts[part][at:at + 1]

    def corrupted(joint, channel):
        def add(patch, totals):
            jr = joint[patch, channel:channel + 1, :]
            ji = joint[patch, 2 + channel:3 + channel, :]
            mr, mi = model[channel, patch, 0], model[channel, patch, 1]
            return totals[0] + (jr * mr - ji * mi), totals[1] + (jr * mi + ji * mr)

        zero = jnp.zeros((TIMES, LANES), F32)
        return lax.fori_loop(0, DIRS, add, (zero, zero), unroll=True)

    for channel in range(2):
        totals = corrupted(joint_true, channel)
        for part in range(2):
            observed[channel, part] = noise[pl.ds(channel * 32 + part, TIMES, stride=2), :] + totals[part]

    def put_energy(patch, _):
        for channel in range(2):
            mr, mi = model[channel, patch, 0], model[channel, patch, 1]
            row = jnp.sum(mr * mr + mi * mi, axis=0, keepdims=True)
            weight = jnp.full((1, LANES), 1.0, F32) * (1.0 - flags[channel].astype(F32))
            for part in range(2):
                at = part * 2 + channel
                energy[patch, at:at + 1, :] = row
                energy[patch, 4 + at:5 + at, :] = weight
        return 0

    lax.fori_loop(0, DIRS, put_energy, 0, unroll=True)

    away = (1 - z_hi) * BL + bl
    for channel in range(2):
        first_out[channel] = start_gains[pl.ds(pl.multiple_of(channel * 128 + away * 8, 8), 8), :]

    neighbours = jnp.where(above, LINE, 0) + jnp.where(below, LINE, 0)
    pl.semaphore_wait(barrier, RING - 1 + LINE - 1 + neighbours)

    sends = []

    def remote(src, dst, send, recv, device):
        return pltpu.make_async_remote_copy(
            src_ref=src, dst_ref=dst, send_sem=send, recv_sem=recv, device_id=device, device_id_type=MESH)

    def to_ring(outgoing, incoming, send, recv):
        copies = []
        for step in range(1, RING):
            other, device = ring(step)
            copy = remote(outgoing.at[other], incoming.at[me], send.at[step], recv.at[step], device)
            copy.start()
            copies.append(copy)
        incoming[me] = outgoing[me]
        sends.extend(copies)
        return copies

    first_copy = remote(first_out, first_in, s_first, r_first, ring(BL)[1])
    first_copy.start()
    sends.append(first_copy)
    energy_copies = to_ring(energy, energy_in, s_energy, r_energy)

    row8 = lax.broadcasted_iota(jnp.int32, (8, LANES), 0)
    is_real = (row8 & 2) == 0

    def from_later(value):
        return pltpu.roll(value, 6, 0)

    def from_earlier(value):
        return pltpu.roll(value, 2, 0)

    def swapped(value):
        return jnp.where(is_real, from_later(value), from_earlier(value))

    def put_ends(gains):
        rows = jnp.concatenate([
            jnp.concatenate([gains[0:4], gains[8:12]], axis=0),
            jnp.concatenate([gains[4:8], gains[12:16]], axis=0)], axis=1)
        high, low = split_two(rows)
        both = jnp.dot(jnp.concatenate([high, low], axis=0), onehot[...], preferred_element_type=F32)
        both = both[0:8] + both[8:16]
        for source in range(BL):
            firsts[source] = both[:, source * 256:source * 256 + LANES]
            seconds[source] = both[:, source * 256 + LANES:source * 256 + 256]

    def to_halves(rows):
        return jnp.concatenate([
            rows[0:4, 0:256], rows[0:4, 256:512], rows[4:8, 0:256], rows[4:8, 256:512]], axis=0)

    here = lax.broadcasted_iota(jnp.int32, (16, 128), 0)
    there = lax.broadcasted_iota(jnp.int32, (16, 128), 1)
    slot = there >> 3
    slot_y = jnp.where(slot < 8, 0, jnp.where(slot < 12, 1, -1))
    slot_z = jnp.where(slot < 8, slot & 1, jnp.where(slot < 12, 1, 0))
    slot_x = jnp.where(slot < 8, slot >> 1, slot & 3)
    apart = (16 * slot_y + 8 * ((here >> 3) - slot_z) + 2 * (x - slot_x) + (here & 1) - (there & 1)).astype(F32)
    reached = jnp.where((here & 6) == (there & 6), jnp.where(jnp.abs(apart) <= REACH, 1.0, 0.0), 0.0)
    smoothing = jnp.exp(-(apart * apart) / (2.0 * SPREAD * SPREAD)) * reached

    def fitted(round_index):
        joint = joint_in.at[round_index]
        for channel in range(2):
            totals = corrupted(joint, channel)
            rest_r = observed[channel, 0] - totals[0]
            rest_i = observed[channel, 1] - totals[1]

            def put_fit(patch, _):
                mr, mi = model[channel, patch, 0], model[channel, patch, 1]
                power = energy[patch, channel:channel + 1, :]
                for part, value in enumerate((mr * rest_r + mi * rest_i, mr * rest_i - mi * rest_r)):
                    at = part * 2 + channel
                    row = jnp.sum(value, axis=0, keepdims=True)
                    fits[round_index, patch, at:at + 1, :] = row + joint[patch, at:at + 1, :] * power
                return 0

            lax.fori_loop(0, DIRS, put_fit, 0, unroll=True)

    inverse = None
    weight_halves = None
    weight_rows = None
    power_rows = []
    for turn in range(ITERS):
        if turn > 0:
            for copy in joint_copies:
                copy.wait_recv()
        fitted(turn)
        fit_copies = to_ring(fits.at[turn], fits_in.at[turn], s_fit.at[turn], r_fit.at[turn])
        if turn == 0:
            first_copy.wait_recv()
            for channel in range(2):
                own = start_gains[pl.ds(pl.multiple_of(channel * 128 + me * 8, 8), 8), :]
                other = first_in[channel]
                for row in range(8):
                    half, lane, part = row // 4, (row // 2) % 2, row % 2
                    at = half * 4 + part * 2 + channel
                    owned[z_hi, at:at + 1, lane * LANES:(lane + 1) * LANES] = own[row:row + 1]
                    owned[1 - z_hi, at:at + 1, lane * LANES:(lane + 1) * LANES] = other[row:row + 1]
            gains_now = owned[...].reshape(16, 256)
            put_ends(gains_now)
            for copy in energy_copies:
                copy.wait_recv()
            for source in range(BL):
                power_rows.append(jnp.concatenate([energy_in[source, 0:4], energy_in[BL + source, 0:4]], axis=0))
            weight_rows = jnp.concatenate([energy_in[0, 4:8], energy_in[BL, 4:8]], axis=0)
            weight_rows = jnp.concatenate([weight_rows] * 4, axis=1)
            weight_halves = to_halves(weight_rows)
        for copy in fit_copies:
            copy.wait_recv()

        columns = []
        for source in range(BL):
            fit = jnp.concatenate([fits_in[turn, source], fits_in[turn, BL + source]], axis=0)
            power = power_rows[source]
            for toward_first in (True, False):
                far = (seconds if toward_first else firsts)[source]
                far_swapped = swapped(far)
                direct = far * fit
                crossed = far_swapped * fit
                if toward_first:
                    numer = jnp.where(is_real, direct - from_later(direct), crossed + from_earlier(crossed))
                else:
                    numer = jnp.where(is_real, direct + from_later(direct), from_earlier(crossed) - crossed)
                denom = (far * far + far_swapped * far_swapped) * power
                high, low = split_two(jnp.concatenate([numer, denom], axis=0))
                columns.append(jnp.concatenate([high, low], axis=0))
        received = lax.dot_general(
            jnp.concatenate(columns, axis=1), onehot[...], (((1,), (1,)), ((), ())), preferred_element_type=F32)
        received = received[0:16] + received[16:32]
        solved = (received[0:8] * weight_rows) / jnp.maximum(received[8:16] * weight_rows, 1.0)
        blended = 0.5 * gains_now + 0.5 * to_halves(solved)
        packed = weight_halves * blended

        width = 384 if turn == 0 else 256
        for z in range(2):
            mixed[turn, 2 * x + z, :, 0:256] = packed[z * 8:z * 8 + 8]
            if turn == 0:
                mixed[turn, 2 * x + z, :, 256:384] = weight_halves[z * 8:z * 8 + 8, 0:LANES]

        def planes(first, count):
            return mixed.at[turn, pl.ds(first, count), :, pl.ds(0, width)]

        line_copies, far_copies = [], []
        for other_x in range(LINE):
            up = remote(planes(2 * x + 1, 1), planes(8 + x, 1), s_mix.at[turn, 3 + other_x],
                        r_mix.at[turn, 4 + x], plane(y + 1, other_x))
            down = remote(planes(2 * x, 1), planes(12 + x, 1), s_mix.at[turn, 7 + other_x],
                          r_mix.at[turn, 8 + x], plane(y - 1, other_x))
            far_copies.append((jnp.logical_and(above, other_x <= x), up))
            far_copies.append((jnp.logical_and(below, other_x >= x), down))
        for step in range(1, LINE):
            copy = remote(planes(2 * x, 2), planes(2 * x, 2), s_mix.at[turn, step - 1], r_mix.at[turn, x],
                          plane(y, lax.rem(x + step, LINE)))
            copy.start()
            line_copies.append(copy)
        for needed, copy in far_copies:
            pl.when(needed)(copy.start)

        for step in range(1, LINE):
            source_x = lax.rem(x + step, LINE)
            remote(planes(2 * source_x, 2), planes(2 * source_x, 2), s_mix.at[turn, step - 1],
                   r_mix.at[turn, source_x], plane(y, source_x)).wait_recv()
        for source_x in range(LINE):
            from_above = remote(planes(12 + source_x, 1), planes(12 + source_x, 1), s_mix.at[turn, 3 + source_x],
                                r_mix.at[turn, 8 + source_x], plane(y + 1, source_x))
            from_below = remote(planes(8 + source_x, 1), planes(8 + source_x, 1), s_mix.at[turn, 7 + source_x],
                                r_mix.at[turn, 4 + source_x], plane(y - 1, source_x))
            pl.when(jnp.logical_and(above, source_x <= x))(from_above.wait_recv)
            pl.when(jnp.logical_and(below, source_x >= x))(from_below.wait_recv)
        summed = jnp.dot(smoothing, mixed[turn, :, :, 0:width].reshape(128, width),
                         precision=lax.Precision.HIGHEST, preferred_element_type=F32)
        if turn == 0:
            inverse = 1.0 / jnp.maximum(summed[:, 256:384], 1.0)
            inverse = jnp.concatenate([inverse, inverse], axis=1)
        gains_now = summed[:, 0:256] * inverse

        put_ends(gains_now)
        for source in range(BL):
            near, far = firsts[source], seconds[source]
            direct = near * far
            crossed = near * swapped(far)
            joint = jnp.where(is_real, direct + from_later(direct), crossed - from_earlier(crossed))
            joint_out[turn, source] = joint[0:4]
            joint_out[turn, BL + source] = joint[4:8]
        joint_copies = to_ring(joint_out.at[turn], joint_in.at[turn + 1], s_joint.at[turn], r_joint.at[turn])

        for copy in line_copies:
            copy.wait_send()
        for needed, copy in far_copies:
            pl.when(needed)(copy.wait_send)

    for z in range(2):
        for channel in range(2):
            for row in range(8):
                half, lane, part = row // 4, (row // 2) % 2, row % 2
                at = z * 8 + half * 4 + part * 2 + channel
                stage[z, channel, row:row + 1, :] = gains_now[at:at + 1, lane * LANES:(lane + 1) * LANES]
    gain_copies = []
    for step in range(1, RING):
        other, device = ring(step)
        copy = remote(stage.at[lax.div(other, BL)], gains_out.at[:, me], s_gain.at[step], r_gain.at[step], device)
        copy.start()
        gain_copies.append(copy)
    sends.extend(gain_copies)
    gains_out[:, me] = stage[z_hi]

    for copy in joint_copies:
        copy.wait_recv()
    for channel in range(2):
        totals = corrupted(joint_in.at[ITERS], channel)
        for part in range(2):
            residual_out[pl.ds(channel * 32 + part, TIMES, stride=2), :] = observed[channel, part] - totals[part]
    for copy in gain_copies:
        copy.wait_recv()
    for copy in sends:
        copy.wait_send()


def local(visibility_noise, baseline_wavelength_coords, station_pair, comp_position, comp_flux,
          comp_spectral, comp_count, true_gains, start_gains, channel_flags):
    vmem = pl.BlockSpec(memory_space=VMEM)
    smem = pl.BlockSpec(memory_space=SMEM)
    dma = pltpu.SemaphoreType.DMA
    params = pl.pallas_call(
        gather_kernel,
        out_shape=jax.ShapeDtypeStruct((BL, 8, LANES), F32),
        in_specs=[vmem, vmem, vmem, smem, vmem],
        out_specs=vmem,
        scratch_shapes=[dma((BL,)), dma((BL,))],
        compiler_params=pltpu.CompilerParams(collective_id=0, has_side_effects=True),
        name="gather_params",
    )(comp_position, comp_flux, comp_spectral, comp_count, station_pair)
    params = params.reshape(BL * 8, LANES)
    model = pl.pallas_call(
        predict_kernel,
        out_shape=jax.ShapeDtypeStruct((2, DIRS, 2, TIMES, LANES), F32),
        in_specs=[smem, vmem],
        out_specs=vmem,
        name="predict",
    )(params, baseline_wavelength_coords)

    def tiles(gains):
        return gains.reshape(2, DIRS, 2, 4, LANES).transpose(0, 1, 3, 2, 4).reshape(2 * DIRS * 8, LANES)

    gains, residual = pl.pallas_call(
        calibrate_kernel,
        out_shape=(jax.ShapeDtypeStruct((2, DIRS, 8, LANES), F32), jax.ShapeDtypeStruct((64, LANES), F32)),
        in_specs=[vmem, vmem, vmem, vmem, vmem, smem],
        out_specs=(vmem, vmem),
        scratch_shapes=[
            pltpu.VMEM((STATIONS, BL * 2 * LANES), BF16),
            pltpu.VMEM((2, 2, TIMES, LANES), F32),
            pltpu.VMEM((DIRS, 4, LANES), F32),
            pltpu.VMEM((BL, 8, LANES), F32),
            pltpu.VMEM((BL, 8, LANES), F32),
            pltpu.VMEM((2, 8, 256), F32),
            pltpu.VMEM((2, 8, LANES), F32),
            pltpu.VMEM((2, 8, LANES), F32),
            pltpu.VMEM((RING, 8, LANES), F32),
            pltpu.VMEM((RING, 8, LANES), F32),
            pltpu.VMEM((ITERS, RING, 4, LANES), F32),
            pltpu.VMEM((ITERS, RING, 4, LANES), F32),
            pltpu.VMEM((ITERS, RING, 4, LANES), F32),
            pltpu.VMEM((ITERS + 1, RING, 4, LANES), F32),
            pltpu.VMEM((ITERS, 16, 8, 384), F32),
            pltpu.VMEM((2, 2, 8, LANES), F32),
            dma(()), dma(()),
            dma((RING,)), dma((RING,)),
            dma((ITERS, RING)), dma((ITERS, RING)),
            dma((ITERS, RING)), dma((ITERS, RING)),
            dma((ITERS, 11)), dma((ITERS, 12)),
            dma((RING,)), dma((RING,)),
        ],
        compiler_params=pltpu.CompilerParams(
            collective_id=1, has_side_effects=True, vmem_limit_bytes=32 * 1024 * 1024),
        name="calibrate",
    )(visibility_noise.reshape(64, LANES), model, params, tiles(true_gains), tiles(start_gains), channel_flags)
    gains = gains.reshape(2, DIRS, 4, 2, LANES).transpose(0, 1, 3, 2, 4).reshape(2, DIRS, 2, STATIONS)
    return gains, residual.reshape(2, TIMES, 2, LANES)


def solution(mesh):
    in_specs = (
        P("freq", None, None, "bl"),
        P(None, None, "bl"),
        P(None, "bl"),
        P("bl", None, None),
        P("bl", None),
        P("bl", None),
        P("bl"),
        P("freq", None, None, None),
        P("freq", None, None, None),
        P("freq"),
    )
    out_specs = (P("freq", None, None, None), P("freq", None, None, "bl"))
    return jax.shard_map(local, mesh=mesh, in_specs=in_specs, out_specs=out_specs, check_vma=False)
```

```python
import jax
import jax.numpy as jnp
from jax import lax
from jax.experimental import pallas as pl
from jax.experimental.pallas import tpu as pltpu
from jax.sharding import PartitionSpec as P

F32 = jnp.float32
BF16 = jnp.bfloat16
MESH = pl.DeviceIdType.MESH
VMEM = pltpu.MemorySpace.VMEM
SMEM = pltpu.MemorySpace.SMEM

BL = 8
LINE = 4
RING = 16
ITERS = 3
DIRS = 16
TIMES = 16
STATIONS = 512
COMPONENTS = 512
LANES = 128
REACH = 8.0
SPREAD = 4.0

SIN_SCALE, SIN_FACTORS = -0.5546349618, (-0.978320908350836, -3.6046909402902565, 5.789750187942454)
COS_SCALE, COS_FACTORS = -1.2221263189, (-0.24999786765951873, -3.0567664626737323, 3.2729900649797434)


def factored(factors, at):
    return (at + factors[0]) * (at * (at + factors[1]) + factors[2])


def split_two(value):
    high = value.astype(BF16)
    low = (value - high.astype(F32)).astype(BF16)
    return high, low


def ratio_of(channel):
    return 0.5 + (channel.astype(F32) + 0.5) / 128.0


def calibrate_kernel(noise_hbm, coords_hbm, pair, position, flux, spectral, count, true_hbm, start_hbm, flags,
                     gains_out, residual_out,
                     noise, coords, true_gains, start_gains, params, ids, params_scalar, ids_scalar, running, model,
                     own_onehot, onehot, observed, joint_true, firsts, seconds, owned, first_out, first_in,
                     energy, energy_in, fits, fits_in, joint_out, joint_in, mixed, stage,
                     s_load, s_param, r_param, s_ids, r_ids,
                     s_first, r_first, s_energy, r_energy, s_fit, r_fit, s_joint, r_joint,
                     s_mix, r_mix, s_gain, r_gain):
    freq = lax.axis_index("freq")
    bl = lax.axis_index("bl")
    y = lax.div(freq, 8)
    z_hi = lax.rem(lax.div(freq, LINE), 2)
    x = lax.rem(freq, LINE)
    me = z_hi * BL + bl
    above, below = y < lax.axis_size("freq") // 8 - 1, y > 0

    def ring(step):
        other = lax.rem(me + step, RING)
        device = {"freq": (y * 2 + lax.div(other, BL)) * LINE + x, "bl": lax.rem(other, BL)}
        return other, device

    def plane(other_y, other_x):
        return {"freq": (other_y * 2 + z_hi) * LINE + other_x, "bl": bl}

    loads = []
    for index, (source, target) in enumerate((
            (true_hbm, true_gains), (start_hbm, start_gains), (noise_hbm, noise), (coords_hbm, coords))):
        copy = pltpu.make_async_copy(source, target, s_load.at[index])
        copy.start()
        loads.append(copy)

    mixed[...] = jnp.zeros(mixed.shape, F32)

    barrier = pltpu.get_barrier_semaphore()
    for step in range(1, RING):
        pl.semaphore_signal(barrier, inc=1, device_id=ring(step)[1], device_id_type=MESH)
    for step in range(1, LINE):
        pl.semaphore_signal(barrier, inc=1, device_id=plane(y, lax.rem(x + step, LINE)), device_id_type=MESH)

    @pl.when(above)
    def _():
        for other_x in range(LINE):
            pl.semaphore_signal(barrier, inc=1, device_id=plane(y + 1, other_x), device_id_type=MESH)

    @pl.when(below)
    def _():
        for other_x in range(LINE):
            pl.semaphore_signal(barrier, inc=1, device_id=plane(y - 1, other_x), device_id_type=MESH)

    def both(values):
        return jnp.concatenate([values[0:1], values[1:2]], axis=1)

    l, m = both(position[:, 0, :]), both(position[:, 1, :])
    square = l * l + m * m
    params[bl, 0:1, :] = l
    params[bl, 1:2, :] = m
    params[bl, 2:3, :] = -square / (1.0 + jnp.sqrt(1.0 - square))
    lane = lax.broadcasted_iota(jnp.int32, (1, LANES), 1)
    lives = jnp.where(lane < 64, count[0], count[1])
    fluxes = jnp.where((lane & 63) < lives, both(flux[...]), 0.0)
    index = both(spectral[...])
    extra = jnp.zeros((1, LANES), F32)
    for channel in range(2):
        ratio = jnp.full((1, LANES), 1.0, F32) * ratio_of(freq * 2 + channel)
        spectrum = fluxes * jnp.exp(index * jnp.log(ratio))
        params[bl, 3 + channel:4 + channel, :] = spectrum
        for half in range(2):
            total = jnp.sum(jnp.where((lane >> 6) == half, spectrum, 0.0), axis=1, keepdims=True)
            extra = jnp.where(lane == half * 2 + channel, total, extra)
    params[bl, 5:6, :] = extra
    ids[bl, 0:2, :] = pair[...]
    ids[bl, 2:3, :] = jnp.where(lane == 0, count[0], count[1])

    station = lax.broadcasted_iota(jnp.int32, (STATIONS, LANES), 0)
    for end in range(2):
        own_onehot[:, end * LANES:(end + 1) * LANES] = jnp.where(station == pair[end:end + 1, :], 1.0, 0.0).astype(BF16)
    for copy in loads:
        copy.wait()

    def local_joint(gains):
        rows = []
        for part in range(2):
            rows.append(jnp.concatenate(
                [gains[pl.ds(tile * 2 + part, 32, stride=8), :] for tile in range(4)], axis=1))
        high, low = split_two(jnp.concatenate(rows, axis=0))
        ends = jnp.dot(jnp.concatenate([high, low], axis=0), own_onehot[...], preferred_element_type=F32)
        ends = ends[0:64] + ends[64:128]
        pr, pi = ends[0:32, 0:LANES], ends[32:64, 0:LANES]
        qr, qi = ends[0:32, LANES:], ends[32:64, LANES:]
        return pr * qr + pi * qi, pi * qr - pr * qi

    for ref, gains in ((joint_true, true_gains), (joint_in.at[0], start_gains)):
        parts = local_joint(gains)
        for channel in range(2):
            for part in range(2):
                for patch in range(DIRS):
                    at = channel * DIRS + patch
                    ref[patch, part * 2 + channel:part * 2 + channel + 1, :] = parts[part][at:at + 1]

    away = (1 - z_hi) * BL + bl
    for channel in range(2):
        first_out[channel] = start_gains[pl.ds(pl.multiple_of(channel * 128 + away * 8, 8), 8), :]

    neighbours = jnp.where(above, LINE, 0) + jnp.where(below, LINE, 0)
    pl.semaphore_wait(barrier, RING - 1 + LINE - 1 + neighbours)

    sends = []

    def remote(src, dst, send, recv, device):
        return pltpu.make_async_remote_copy(
            src_ref=src, dst_ref=dst, send_sem=send, recv_sem=recv, device_id=device, device_id_type=MESH)

    param_copies = []
    for step in (4, 3, 5, 2, 6, 1, 7):
        device = {"bl": lax.rem(bl + step, BL)}
        for outgoing, send, recv in ((params, s_param, r_param), (ids, s_ids, r_ids)):
            copy = remote(outgoing.at[bl], outgoing.at[bl], send.at[step], recv.at[step], device)
            copy.start()
            param_copies.append(copy)
    sends.extend(param_copies)
    first_copy = remote(first_out, first_in, s_first, r_first, ring(BL)[1])
    first_copy.start()
    sends.append(first_copy)
    for copy in param_copies:
        copy.wait_recv()
    scalars = [pltpu.make_async_copy(params, params_scalar, s_load.at[4]),
               pltpu.make_async_copy(ids, ids_scalar, s_load.at[5])]
    for copy in scalars:
        copy.start()
    for copy in scalars:
        copy.wait()

    ratio_zero, ratio_one = ratio_of(freq * 2), ratio_of(freq * 2 + 1)
    relative = ratio_one / ratio_zero
    u, v, w = coords[0] * ratio_zero, coords[1] * ratio_zero, coords[2] * ratio_zero

    def lives_of(patch):
        return ids_scalar[patch >> 1, 2, patch & 1]

    def one_component(component, state):
        sums, (patch, slot, live) = list(state[0:4]), state[4:7]
        device, column = patch >> 1, (patch & 1) * 64 + slot
        delay = (u * params_scalar[device, 0, column] + v * params_scalar[device, 1, column]
                 + w * params_scalar[device, 2, column])
        keep = jnp.where(slot == 0, 0.0, 1.0)
        for channel, turns in enumerate((delay, delay * relative)):
            turns = turns - jnp.round(turns)
            square = turns * turns
            sine = turns * factored(SIN_FACTORS, square)
            scaled = sine * params_scalar[device, 3 + channel, column]
            sums[2 * channel] = sums[2 * channel] * keep + scaled * sine
            sums[2 * channel + 1] = sums[2 * channel + 1] * keep + scaled * factored(COS_FACTORS, square)
        for place in range(4):
            running[component, place] = sums[place]
        done = slot + 1 >= live
        patch = jnp.minimum(patch + jnp.where(done, 1, 0), DIRS - 1)
        slot = jnp.where(done, 0, slot + 1)
        return (*sums, patch, slot, lives_of(patch))

    zero = jnp.zeros((TIMES, LANES), F32)
    start = jnp.int32(0)
    lax.fori_loop(0, COMPONENTS, one_component, (zero,) * 4 + (start, start, lives_of(start)), unroll=16)

    def finish_patch(patch, end):
        end = end + lives_of(patch)
        last = jnp.clip(end - 1, 0, COMPONENTS - 1)
        for channel in range(2):
            total = params_scalar[patch >> 1, 5, (patch & 1) * 2 + channel]
            model[channel, patch, 0] = total - (2.0 * SIN_SCALE * SIN_SCALE) * running[last, 2 * channel]
            model[channel, patch, 1] = (-2.0 * SIN_SCALE * COS_SCALE) * running[last, 2 * channel + 1]
        return end

    lax.fori_loop(0, DIRS, finish_patch, start, unroll=True)

    def corrupted(joint, channel):
        def add(patch, totals):
            jr = joint[patch, channel:channel + 1, :]
            ji = joint[patch, 2 + channel:3 + channel, :]
            mr, mi = model[channel, patch, 0], model[channel, patch, 1]
            return totals[0] + (jr * mr - ji * mi), totals[1] + (jr * mi + ji * mr)

        zero = jnp.zeros((TIMES, LANES), F32)
        return lax.fori_loop(0, DIRS, add, (zero, zero), unroll=True)

    for channel in range(2):
        totals = corrupted(joint_true, channel)
        for part in range(2):
            observed[channel, part] = noise[pl.ds(channel * 32 + part, TIMES, stride=2), :] + totals[part]

    def put_energy(patch, _):
        for channel in range(2):
            mr, mi = model[channel, patch, 0], model[channel, patch, 1]
            row = jnp.sum(mr * mr + mi * mi, axis=0, keepdims=True)
            weight = jnp.full((1, LANES), 1.0, F32) * (1.0 - flags[channel].astype(F32))
            for part in range(2):
                at = part * 2 + channel
                energy[patch, at:at + 1, :] = row
                energy[patch, 4 + at:5 + at, :] = weight
        return 0

    lax.fori_loop(0, DIRS, put_energy, 0, unroll=True)

    def to_ring(outgoing, incoming, send, recv):
        copies = []
        for step in range(1, RING):
            other, device = ring(step)
            copy = remote(outgoing.at[other], incoming.at[me], send.at[step], recv.at[step], device)
            copy.start()
            copies.append(copy)
        incoming[me] = outgoing[me]
        sends.extend(copies)
        return copies

    energy_copies = to_ring(energy, energy_in, s_energy, r_energy)

    row8 = lax.broadcasted_iota(jnp.int32, (8, LANES), 0)
    is_real = (row8 & 2) == 0

    def from_later(value):
        return pltpu.roll(value, 6, 0)

    def from_earlier(value):
        return pltpu.roll(value, 2, 0)

    def swapped(value):
        return jnp.where(is_real, from_later(value), from_earlier(value))

    def put_ends(gains):
        rows = jnp.concatenate([
            jnp.concatenate([gains[0:4], gains[8:12]], axis=0),
            jnp.concatenate([gains[4:8], gains[12:16]], axis=0)], axis=1)
        high, low = split_two(rows)
        both = jnp.dot(jnp.concatenate([high, low], axis=0), onehot[...], preferred_element_type=F32)
        both = both[0:8] + both[8:16]
        for source in range(BL):
            firsts[source] = both[:, source * 256:source * 256 + LANES]
            seconds[source] = both[:, source * 256 + LANES:source * 256 + 256]

    def to_halves(rows):
        return jnp.concatenate([
            rows[0:4, 0:256], rows[0:4, 256:512], rows[4:8, 0:256], rows[4:8, 256:512]], axis=0)

    here = lax.broadcasted_iota(jnp.int32, (16, 128), 0)
    there = lax.broadcasted_iota(jnp.int32, (16, 128), 1)
    slot = there >> 3
    slot_y = jnp.where(slot < 8, 0, jnp.where(slot < 12, 1, -1))
    slot_z = jnp.where(slot < 8, slot & 1, jnp.where(slot < 12, 1, 0))
    slot_x = jnp.where(slot < 8, slot >> 1, slot & 3)
    apart = (16 * slot_y + 8 * ((here >> 3) - slot_z) + 2 * (x - slot_x) + (here & 1) - (there & 1)).astype(F32)
    reached = jnp.where((here & 6) == (there & 6), jnp.where(jnp.abs(apart) <= REACH, 1.0, 0.0), 0.0)
    smoothing = jnp.exp(-(apart * apart) / (2.0 * SPREAD * SPREAD)) * reached

    def fitted(round_index):
        joint = joint_in.at[round_index]
        for channel in range(2):
            totals = corrupted(joint, channel)
            rest_r = observed[channel, 0] - totals[0]
            rest_i = observed[channel, 1] - totals[1]

            def put_fit(patch, _):
                mr, mi = model[channel, patch, 0], model[channel, patch, 1]
                power = energy[patch, channel:channel + 1, :]
                for part, value in enumerate((mr * rest_r + mi * rest_i, mr * rest_i - mi * rest_r)):
                    at = part * 2 + channel
                    row = jnp.sum(value, axis=0, keepdims=True)
                    fits[round_index, patch, at:at + 1, :] = row + joint[patch, at:at + 1, :] * power
                return 0

            lax.fori_loop(0, DIRS, put_fit, 0, unroll=True)

    inverse = None
    weight_halves = None
    weight_rows = None
    power_rows = []
    for turn in range(ITERS):
        if turn > 0:
            for copy in joint_copies:
                copy.wait_recv()
        fitted(turn)
        fit_copies = to_ring(fits.at[turn], fits_in.at[turn], s_fit.at[turn], r_fit.at[turn])
        if turn == 0:
            for source in range(BL):
                for end in range(2):
                    row = ids[source, end:end + 1, :]
                    start = (source * 2 + end) * LANES
                    onehot[:, start:start + LANES] = jnp.where(station == row, 1.0, 0.0).astype(BF16)
            first_copy.wait_recv()
            for channel in range(2):
                own = start_gains[pl.ds(pl.multiple_of(channel * 128 + me * 8, 8), 8), :]
                other = first_in[channel]
                for row in range(8):
                    half, lane, part = row // 4, (row // 2) % 2, row % 2
                    at = half * 4 + part * 2 + channel
                    owned[z_hi, at:at + 1, lane * LANES:(lane + 1) * LANES] = own[row:row + 1]
                    owned[1 - z_hi, at:at + 1, lane * LANES:(lane + 1) * LANES] = other[row:row + 1]
            gains_now = owned[...].reshape(16, 256)
            put_ends(gains_now)
            for copy in energy_copies:
                copy.wait_recv()
            for source in range(BL):
                power_rows.append(jnp.concatenate([energy_in[source, 0:4], energy_in[BL + source, 0:4]], axis=0))
            weight_rows = jnp.concatenate([energy_in[0, 4:8], energy_in[BL, 4:8]], axis=0)
            weight_rows = jnp.concatenate([weight_rows] * 4, axis=1)
            weight_halves = to_halves(weight_rows)
        for copy in fit_copies:
            copy.wait_recv()

        columns = []
        for source in range(BL):
            fit = jnp.concatenate([fits_in[turn, source], fits_in[turn, BL + source]], axis=0)
            power = power_rows[source]
            for toward_first in (True, False):
                far = (seconds if toward_first else firsts)[source]
                far_swapped = swapped(far)
                direct = far * fit
                crossed = far_swapped * fit
                if toward_first:
                    numer = jnp.where(is_real, direct - from_later(direct), crossed + from_earlier(crossed))
                else:
                    numer = jnp.where(is_real, direct + from_later(direct), from_earlier(crossed) - crossed)
                denom = (far * far + far_swapped * far_swapped) * power
                high, low = split_two(jnp.concatenate([numer, denom], axis=0))
                columns.append(jnp.concatenate([high, low], axis=0))
        received = lax.dot_general(
            jnp.concatenate(columns, axis=1), onehot[...], (((1,), (1,)), ((), ())), preferred_element_type=F32)
        received = received[0:16] + received[16:32]
        solved = (received[0:8] * weight_rows) / jnp.maximum(received[8:16] * weight_rows, 1.0)
        blended = 0.5 * gains_now + 0.5 * to_halves(solved)
        packed = weight_halves * blended

        width = 384 if turn == 0 else 256
        for z in range(2):
            mixed[turn, 2 * x + z, :, 0:256] = packed[z * 8:z * 8 + 8]
            if turn == 0:
                mixed[turn, 2 * x + z, :, 256:384] = weight_halves[z * 8:z * 8 + 8, 0:LANES]

        def planes(first, count):
            return mixed.at[turn, pl.ds(first, count), :, pl.ds(0, width)]

        line_copies, far_copies = [], []
        for other_x in range(LINE):
            up = remote(planes(2 * x + 1, 1), planes(8 + x, 1), s_mix.at[turn, 3 + other_x],
                        r_mix.at[turn, 4 + x], plane(y + 1, other_x))
            down = remote(planes(2 * x, 1), planes(12 + x, 1), s_mix.at[turn, 7 + other_x],
                          r_mix.at[turn, 8 + x], plane(y - 1, other_x))
            far_copies.append((jnp.logical_and(above, other_x <= x), up))
            far_copies.append((jnp.logical_and(below, other_x >= x), down))
        for step in range(1, LINE):
            copy = remote(planes(2 * x, 2), planes(2 * x, 2), s_mix.at[turn, step - 1], r_mix.at[turn, x],
                          plane(y, lax.rem(x + step, LINE)))
            copy.start()
            line_copies.append(copy)
        for needed, copy in far_copies:
            pl.when(needed)(copy.start)

        for step in range(1, LINE):
            source_x = lax.rem(x + step, LINE)
            remote(planes(2 * source_x, 2), planes(2 * source_x, 2), s_mix.at[turn, step - 1],
                   r_mix.at[turn, source_x], plane(y, source_x)).wait_recv()
        for source_x in range(LINE):
            from_above = remote(planes(12 + source_x, 1), planes(12 + source_x, 1), s_mix.at[turn, 3 + source_x],
                                r_mix.at[turn, 8 + source_x], plane(y + 1, source_x))
            from_below = remote(planes(8 + source_x, 1), planes(8 + source_x, 1), s_mix.at[turn, 7 + source_x],
                                r_mix.at[turn, 4 + source_x], plane(y - 1, source_x))
            pl.when(jnp.logical_and(above, source_x <= x))(from_above.wait_recv)
            pl.when(jnp.logical_and(below, source_x >= x))(from_below.wait_recv)
        summed = jnp.dot(smoothing, mixed[turn, :, :, 0:width].reshape(128, width),
                         precision=lax.Precision.HIGHEST, preferred_element_type=F32)
        if turn == 0:
            inverse = 1.0 / jnp.maximum(summed[:, 256:384], 1.0)
            inverse = jnp.concatenate([inverse, inverse], axis=1)
        gains_now = summed[:, 0:256] * inverse

        put_ends(gains_now)
        for source in range(BL):
            near, far = firsts[source], seconds[source]
            direct = near * far
            crossed = near * swapped(far)
            joint = jnp.where(is_real, direct + from_later(direct), crossed - from_earlier(crossed))
            joint_out[turn, source] = joint[0:4]
            joint_out[turn, BL + source] = joint[4:8]
        joint_copies = to_ring(joint_out.at[turn], joint_in.at[turn + 1], s_joint.at[turn], r_joint.at[turn])

        for copy in line_copies:
            copy.wait_send()
        for needed, copy in far_copies:
            pl.when(needed)(copy.wait_send)

    for z in range(2):
        for channel in range(2):
            for row in range(8):
                half, lane, part = row // 4, (row // 2) % 2, row % 2
                at = z * 8 + half * 4 + part * 2 + channel
                stage[z, channel, row:row + 1, :] = gains_now[at:at + 1, lane * LANES:(lane + 1) * LANES]
    gain_copies = []
    for step in range(1, RING):
        other, device = ring(step)
        copy = remote(stage.at[lax.div(other, BL)], gains_out.at[:, me], s_gain.at[step], r_gain.at[step], device)
        copy.start()
        gain_copies.append(copy)
    sends.extend(gain_copies)
    gains_out[:, me] = stage[z_hi]

    for copy in joint_copies:
        copy.wait_recv()
    for channel in range(2):
        totals = corrupted(joint_in.at[ITERS], channel)
        for part in range(2):
            residual_out[pl.ds(channel * 32 + part, TIMES, stride=2), :] = observed[channel, part] - totals[part]
    for copy in gain_copies:
        copy.wait_recv()
    for copy in sends:
        copy.wait_send()


def local(visibility_noise, baseline_wavelength_coords, station_pair, comp_position, comp_flux,
          comp_spectral, comp_count, true_gains, start_gains, channel_flags):
    vmem = pl.BlockSpec(memory_space=VMEM)
    smem = pl.BlockSpec(memory_space=SMEM)
    anywhere = pl.BlockSpec(memory_space=pltpu.MemorySpace.HBM)
    dma = pltpu.SemaphoreType.DMA
    def tiles(gains):
        return gains.reshape(2, DIRS, 2, 4, LANES).transpose(0, 1, 3, 2, 4).reshape(2 * DIRS * 8, LANES)

    gains, residual = pl.pallas_call(
        calibrate_kernel,
        out_shape=(jax.ShapeDtypeStruct((2, DIRS, 8, LANES), F32), jax.ShapeDtypeStruct((64, LANES), F32)),
        in_specs=[anywhere, anywhere, vmem, vmem, vmem, vmem, smem, anywhere, anywhere, smem],
        out_specs=(vmem, vmem),
        scratch_shapes=[
            pltpu.VMEM((64, LANES), F32),
            pltpu.VMEM((3, TIMES, LANES), F32),
            pltpu.VMEM((256, LANES), F32),
            pltpu.VMEM((256, LANES), F32),
            pltpu.VMEM((BL, 8, LANES), F32),
            pltpu.VMEM((BL, 8, LANES), jnp.int32),
            pltpu.SMEM((BL, 8, LANES), F32),
            pltpu.SMEM((BL, 8, LANES), jnp.int32),
            pltpu.VMEM((COMPONENTS, 4, TIMES, LANES), F32),
            pltpu.VMEM((2, DIRS, 2, TIMES, LANES), F32),
            pltpu.VMEM((STATIONS, 2 * LANES), BF16),
            pltpu.VMEM((STATIONS, BL * 2 * LANES), BF16),
            pltpu.VMEM((2, 2, TIMES, LANES), F32),
            pltpu.VMEM((DIRS, 4, LANES), F32),
            pltpu.VMEM((BL, 8, LANES), F32),
            pltpu.VMEM((BL, 8, LANES), F32),
            pltpu.VMEM((2, 8, 256), F32),
            pltpu.VMEM((2, 8, LANES), F32),
            pltpu.VMEM((2, 8, LANES), F32),
            pltpu.VMEM((RING, 8, LANES), F32),
            pltpu.VMEM((RING, 8, LANES), F32),
            pltpu.VMEM((ITERS, RING, 4, LANES), F32),
            pltpu.VMEM((ITERS, RING, 4, LANES), F32),
            pltpu.VMEM((ITERS, RING, 4, LANES), F32),
            pltpu.VMEM((ITERS + 1, RING, 4, LANES), F32),
            pltpu.VMEM((ITERS, 16, 8, 384), F32),
            pltpu.VMEM((2, 2, 8, LANES), F32),
            dma((6,)), dma((BL,)), dma((BL,)), dma((BL,)), dma((BL,)),
            dma(()), dma(()),
            dma((RING,)), dma((RING,)),
            dma((ITERS, RING)), dma((ITERS, RING)),
            dma((ITERS, RING)), dma((ITERS, RING)),
            dma((ITERS, 11)), dma((ITERS, 12)),
            dma((RING,)), dma((RING,)),
        ],
        compiler_params=pltpu.CompilerParams(
            collective_id=0, has_side_effects=True, vmem_limit_bytes=56 * 1024 * 1024),
        name="calibrate",
    )(visibility_noise.reshape(64, LANES), baseline_wavelength_coords, station_pair, comp_position, comp_flux,
      comp_spectral, comp_count, tiles(true_gains), tiles(start_gains), channel_flags)
    gains = gains.reshape(2, DIRS, 4, 2, LANES).transpose(0, 1, 3, 2, 4).reshape(2, DIRS, 2, STATIONS)
    return gains, residual.reshape(2, TIMES, 2, LANES)


def solution(mesh):
    in_specs = (
        P("freq", None, None, "bl"),
        P(None, None, "bl"),
        P(None, "bl"),
        P("bl", None, None),
        P("bl", None),
        P("bl", None),
        P("bl"),
        P("freq", None, None, None),
        P("freq", None, None, None),
        P("freq"),
    )
    out_specs = (P("freq", None, None, None), P("freq", None, None, "bl"))
    return jax.shard_map(local, mesh=mesh, in_specs=in_specs, out_specs=out_specs, check_vma=False)
```

```python
import jax
import jax.numpy as jnp
from jax import lax
from jax.experimental import pallas as pl
from jax.experimental.pallas import tpu as pltpu
from jax.sharding import PartitionSpec as P

F32 = jnp.float32
BF16 = jnp.bfloat16
MESH = pl.DeviceIdType.MESH
VMEM = pltpu.MemorySpace.VMEM
SMEM = pltpu.MemorySpace.SMEM

FAR_FIRST = (8, 7, 9, 6, 10, 5, 11, 4, 12, 3, 13, 2, 14, 1, 15)
BL = 8
LINE = 4
RING = 16
ITERS = 3
DIRS = 16
TIMES = 16
STATIONS = 512
COMPONENTS = 512
LANES = 128
REACH = 8.0
SPREAD = 4.0

SIN_SCALE, SIN_FACTORS = -0.5546349618, (-0.978320908350836, -3.6046909402902565, 5.789750187942454)
COS_SCALE, COS_FACTORS = -1.2221263189, (-0.24999786765951873, -3.0567664626737323, 3.2729900649797434)


def factored(factors, at):
    return (at + factors[0]) * (at * (at + factors[1]) + factors[2])


def split_two(value):
    high = value.astype(BF16)
    low = (value - high.astype(F32)).astype(BF16)
    return high, low


def ratio_of(channel):
    return 0.5 + (channel.astype(F32) + 0.5) / 128.0


def calibrate_kernel(noise_hbm, coords_hbm, pair, position, flux, spectral, count, true_hbm, start_hbm, flags,
                     gains_out, residual_out,
                     noise, coords, true_gains, start_gains, params, ids, params_scalar, ids_scalar, running, model,
                     own_onehot, onehot, observed, joint_true, firsts, seconds, owned, first_out, first_in,
                     energy, energy_in, fits, fits_in, joint_out, joint_in, mixed, stage,
                     s_load, s_param, r_param, s_ids, r_ids,
                     s_first, r_first, s_energy, r_energy, s_fit, r_fit, s_joint, r_joint,
                     s_mix, r_mix, s_gain, r_gain):
    freq = lax.axis_index("freq")
    bl = lax.axis_index("bl")
    y = lax.div(freq, 8)
    z_hi = lax.rem(lax.div(freq, LINE), 2)
    x = lax.rem(freq, LINE)
    me = z_hi * BL + bl
    above, below = y < lax.axis_size("freq") // 8 - 1, y > 0

    def ring(step):
        other = lax.rem(me + step, RING)
        device = {"freq": (y * 2 + lax.div(other, BL)) * LINE + x, "bl": lax.rem(other, BL)}
        return other, device

    def plane(other_y, other_x):
        return {"freq": (other_y * 2 + z_hi) * LINE + other_x, "bl": bl}

    loads = []
    for index, (source, target) in enumerate((
            (true_hbm, true_gains), (start_hbm, start_gains), (noise_hbm, noise), (coords_hbm, coords))):
        copy = pltpu.make_async_copy(source, target, s_load.at[index])
        copy.start()
        loads.append(copy)

    mixed[...] = jnp.zeros(mixed.shape, F32)

    barrier = pltpu.get_barrier_semaphore()
    for step in range(1, RING):
        pl.semaphore_signal(barrier, inc=1, device_id=ring(step)[1], device_id_type=MESH)
    for step in range(1, LINE):
        pl.semaphore_signal(barrier, inc=1, device_id=plane(y, lax.rem(x + step, LINE)), device_id_type=MESH)

    @pl.when(above)
    def _():
        for other_x in range(LINE):
            pl.semaphore_signal(barrier, inc=1, device_id=plane(y + 1, other_x), device_id_type=MESH)

    @pl.when(below)
    def _():
        for other_x in range(LINE):
            pl.semaphore_signal(barrier, inc=1, device_id=plane(y - 1, other_x), device_id_type=MESH)

    def both(values):
        return jnp.concatenate([values[0:1], values[1:2]], axis=1)

    l, m = both(position[:, 0, :]), both(position[:, 1, :])
    square = l * l + m * m
    params[bl, 0:1, :] = l
    params[bl, 1:2, :] = m
    params[bl, 2:3, :] = -square / (1.0 + jnp.sqrt(1.0 - square))
    lane = lax.broadcasted_iota(jnp.int32, (1, LANES), 1)
    lives = jnp.where(lane < 64, count[0], count[1])
    fluxes = jnp.where((lane & 63) < lives, both(flux[...]), 0.0)
    index = both(spectral[...])
    extra = jnp.zeros((1, LANES), F32)
    for channel in range(2):
        ratio = jnp.full((1, LANES), 1.0, F32) * ratio_of(freq * 2 + channel)
        spectrum = fluxes * jnp.exp(index * jnp.log(ratio))
        params[bl, 3 + channel:4 + channel, :] = spectrum
        for half in range(2):
            total = jnp.sum(jnp.where((lane >> 6) == half, spectrum, 0.0), axis=1, keepdims=True)
            extra = jnp.where(lane == half * 2 + channel, total, extra)
    params[bl, 5:6, :] = extra
    ids[bl, 0:2, :] = pair[...]
    ids[bl, 2:3, :] = jnp.where(lane == 0, count[0], count[1])

    station = lax.broadcasted_iota(jnp.int32, (STATIONS, LANES), 0)
    for end in range(2):
        own_onehot[:, end * LANES:(end + 1) * LANES] = jnp.where(station == pair[end:end + 1, :], 1.0, 0.0).astype(BF16)
    for copy in loads:
        copy.wait()

    def local_joint(gains):
        rows = []
        for part in range(2):
            rows.append(jnp.concatenate(
                [gains[pl.ds(tile * 2 + part, 32, stride=8), :] for tile in range(4)], axis=1))
        high, low = split_two(jnp.concatenate(rows, axis=0))
        ends = jnp.dot(jnp.concatenate([high, low], axis=0), own_onehot[...], preferred_element_type=F32)
        ends = ends[0:64] + ends[64:128]
        pr, pi = ends[0:32, 0:LANES], ends[32:64, 0:LANES]
        qr, qi = ends[0:32, LANES:], ends[32:64, LANES:]
        return pr * qr + pi * qi, pi * qr - pr * qi

    for ref, gains in ((joint_true, true_gains), (joint_in.at[0], start_gains)):
        parts = local_joint(gains)
        for channel in range(2):
            for part in range(2):
                for patch in range(DIRS):
                    at = channel * DIRS + patch
                    ref[patch, part * 2 + channel:part * 2 + channel + 1, :] = parts[part][at:at + 1]

    away = (1 - z_hi) * BL + bl
    for channel in range(2):
        first_out[channel] = start_gains[pl.ds(pl.multiple_of(channel * 128 + away * 8, 8), 8), :]

    neighbours = jnp.where(above, LINE, 0) + jnp.where(below, LINE, 0)
    pl.semaphore_wait(barrier, RING - 1 + LINE - 1 + neighbours)

    sends = []

    def remote(src, dst, send, recv, device):
        return pltpu.make_async_remote_copy(
            src_ref=src, dst_ref=dst, send_sem=send, recv_sem=recv, device_id=device, device_id_type=MESH)

    param_copies = []
    for step in (4, 3, 5, 2, 6, 1, 7):
        device = {"bl": lax.rem(bl + step, BL)}
        for outgoing, send, recv in ((params, s_param, r_param), (ids, s_ids, r_ids)):
            copy = remote(outgoing.at[bl], outgoing.at[bl], send.at[step], recv.at[step], device)
            copy.start()
            param_copies.append(copy)
    sends.extend(param_copies)
    first_copy = remote(first_out, first_in, s_first, r_first, ring(BL)[1])
    first_copy.start()
    sends.append(first_copy)
    for copy in param_copies:
        copy.wait_recv()
    scalars = [pltpu.make_async_copy(params, params_scalar, s_load.at[4]),
               pltpu.make_async_copy(ids, ids_scalar, s_load.at[5])]
    for copy in scalars:
        copy.start()
    for copy in scalars:
        copy.wait()

    ratio_zero, ratio_one = ratio_of(freq * 2), ratio_of(freq * 2 + 1)
    relative = ratio_one / ratio_zero
    u, v, w = coords[0] * ratio_zero, coords[1] * ratio_zero, coords[2] * ratio_zero

    def lives_of(patch):
        return ids_scalar[patch >> 1, 2, patch & 1]

    def one_component(component, state):
        sums, (patch, slot, live) = list(state[0:4]), state[4:7]
        device, column = patch >> 1, (patch & 1) * 64 + slot
        delay = (u * params_scalar[device, 0, column] + v * params_scalar[device, 1, column]
                 + w * params_scalar[device, 2, column])
        keep = jnp.where(slot == 0, 0.0, 1.0)
        for channel, turns in enumerate((delay, delay * relative)):
            turns = turns - jnp.round(turns)
            square = turns * turns
            sine = turns * factored(SIN_FACTORS, square)
            scaled = sine * params_scalar[device, 3 + channel, column]
            sums[2 * channel] = sums[2 * channel] * keep + scaled * sine
            sums[2 * channel + 1] = sums[2 * channel + 1] * keep + scaled * factored(COS_FACTORS, square)
        for place in range(4):
            running[component, place] = sums[place]
        done = slot + 1 >= live
        patch = jnp.minimum(patch + jnp.where(done, 1, 0), DIRS - 1)
        slot = jnp.where(done, 0, slot + 1)
        return (*sums, patch, slot, lives_of(patch))

    zero = jnp.zeros((TIMES, LANES), F32)
    start = jnp.int32(0)
    lax.fori_loop(0, COMPONENTS, one_component, (zero,) * 4 + (start, start, lives_of(start)), unroll=16)

    def finish_patch(patch, end):
        end = end + lives_of(patch)
        last = jnp.clip(end - 1, 0, COMPONENTS - 1)
        for channel in range(2):
            total = params_scalar[patch >> 1, 5, (patch & 1) * 2 + channel]
            model[channel, patch, 0] = total - (2.0 * SIN_SCALE * SIN_SCALE) * running[last, 2 * channel]
            model[channel, patch, 1] = (-2.0 * SIN_SCALE * COS_SCALE) * running[last, 2 * channel + 1]
        return end

    lax.fori_loop(0, DIRS, finish_patch, start, unroll=True)

    def corrupted(joint, channel):
        def add(patch, totals):
            jr = joint[patch, channel:channel + 1, :]
            ji = joint[patch, 2 + channel:3 + channel, :]
            mr, mi = model[channel, patch, 0], model[channel, patch, 1]
            return totals[0] + (jr * mr - ji * mi), totals[1] + (jr * mi + ji * mr)

        zero = jnp.zeros((TIMES, LANES), F32)
        return lax.fori_loop(0, DIRS, add, (zero, zero), unroll=True)

    for channel in range(2):
        totals = corrupted(joint_true, channel)
        for part in range(2):
            observed[channel, part] = noise[pl.ds(channel * 32 + part, TIMES, stride=2), :] + totals[part]

    def put_energy(patch, _):
        for channel in range(2):
            mr, mi = model[channel, patch, 0], model[channel, patch, 1]
            row = jnp.sum(mr * mr + mi * mi, axis=0, keepdims=True)
            weight = jnp.full((1, LANES), 1.0, F32) * (1.0 - flags[channel].astype(F32))
            for part in range(2):
                at = part * 2 + channel
                energy[patch, at:at + 1, :] = row
                energy[patch, 4 + at:5 + at, :] = weight
        return 0

    lax.fori_loop(0, DIRS, put_energy, 0, unroll=True)

    def to_ring(outgoing, incoming, send, recv):
        copies = []
        for step in FAR_FIRST:
            other, device = ring(step)
            copy = remote(outgoing.at[other], incoming.at[me], send.at[step], recv.at[step], device)
            copy.start()
            copies.append(copy)
        incoming[me] = outgoing[me]
        sends.extend(copies)
        return copies

    energy_copies = to_ring(energy, energy_in, s_energy, r_energy)

    row8 = lax.broadcasted_iota(jnp.int32, (8, LANES), 0)
    is_real = (row8 & 2) == 0

    def from_later(value):
        return pltpu.roll(value, 6, 0)

    def from_earlier(value):
        return pltpu.roll(value, 2, 0)

    def swapped(value):
        return jnp.where(is_real, from_later(value), from_earlier(value))

    def put_ends(gains):
        rows = jnp.concatenate([
            jnp.concatenate([gains[0:4], gains[8:12]], axis=0),
            jnp.concatenate([gains[4:8], gains[12:16]], axis=0)], axis=1)
        high, low = split_two(rows)
        both = jnp.dot(jnp.concatenate([high, low], axis=0), onehot[...], preferred_element_type=F32)
        both = both[0:8] + both[8:16]
        for source in range(BL):
            firsts[source] = both[:, source * 256:source * 256 + LANES]
            seconds[source] = both[:, source * 256 + LANES:source * 256 + 256]

    def to_halves(rows):
        return jnp.concatenate([
            rows[0:4, 0:256], rows[0:4, 256:512], rows[4:8, 0:256], rows[4:8, 256:512]], axis=0)

    here = lax.broadcasted_iota(jnp.int32, (16, 128), 0)
    there = lax.broadcasted_iota(jnp.int32, (16, 128), 1)
    slot = there >> 3
    slot_y = jnp.where(slot < 8, 0, jnp.where(slot < 12, 1, -1))
    slot_z = jnp.where(slot < 8, slot & 1, jnp.where(slot < 12, 1, 0))
    slot_x = jnp.where(slot < 8, slot >> 1, slot & 3)
    apart = (16 * slot_y + 8 * ((here >> 3) - slot_z) + 2 * (x - slot_x) + (here & 1) - (there & 1)).astype(F32)
    reached = jnp.where((here & 6) == (there & 6), jnp.where(jnp.abs(apart) <= REACH, 1.0, 0.0), 0.0)
    smoothing = jnp.exp(-(apart * apart) / (2.0 * SPREAD * SPREAD)) * reached

    def fitted(round_index):
        joint = joint_in.at[round_index]
        for channel in range(2):
            totals = corrupted(joint, channel)
            rest_r = observed[channel, 0] - totals[0]
            rest_i = observed[channel, 1] - totals[1]

            def put_fit(patch, _):
                mr, mi = model[channel, patch, 0], model[channel, patch, 1]
                power = energy[patch, channel:channel + 1, :]
                for part, value in enumerate((mr * rest_r + mi * rest_i, mr * rest_i - mi * rest_r)):
                    at = part * 2 + channel
                    row = jnp.sum(value, axis=0, keepdims=True)
                    fits[round_index, patch, at:at + 1, :] = row + joint[patch, at:at + 1, :] * power
                return 0

            lax.fori_loop(0, DIRS, put_fit, 0, unroll=True)

    smoothing_high, smoothing_low = split_two(smoothing)
    smoothing_both = jnp.concatenate([smoothing_high, smoothing_low], axis=0)

    inverse = None
    weight_halves = None
    weight_rows = None
    power_rows = []
    for turn in range(ITERS):
        if turn > 0:
            for copy in joint_copies:
                copy.wait_recv()
        fitted(turn)
        fit_copies = to_ring(fits.at[turn], fits_in.at[turn], s_fit.at[turn], r_fit.at[turn])
        if turn == 0:
            for source in range(BL):
                for end in range(2):
                    row = ids[source, end:end + 1, :]
                    start = (source * 2 + end) * LANES
                    onehot[:, start:start + LANES] = jnp.where(station == row, 1.0, 0.0).astype(BF16)
            first_copy.wait_recv()
            for channel in range(2):
                own = start_gains[pl.ds(pl.multiple_of(channel * 128 + me * 8, 8), 8), :]
                other = first_in[channel]
                for row in range(8):
                    half, lane, part = row // 4, (row // 2) % 2, row % 2
                    at = half * 4 + part * 2 + channel
                    owned[z_hi, at:at + 1, lane * LANES:(lane + 1) * LANES] = own[row:row + 1]
                    owned[1 - z_hi, at:at + 1, lane * LANES:(lane + 1) * LANES] = other[row:row + 1]
            gains_now = owned[...].reshape(16, 256)
            put_ends(gains_now)
            for copy in energy_copies:
                copy.wait_recv()
            for source in range(BL):
                power_rows.append(jnp.concatenate([energy_in[source, 0:4], energy_in[BL + source, 0:4]], axis=0))
            weight_rows = jnp.concatenate([energy_in[0, 4:8], energy_in[BL, 4:8]], axis=0)
            weight_rows = jnp.concatenate([weight_rows] * 4, axis=1)
            weight_halves = to_halves(weight_rows)
        for copy in fit_copies:
            copy.wait_recv()

        columns = []
        for source in range(BL):
            fit = jnp.concatenate([fits_in[turn, source], fits_in[turn, BL + source]], axis=0)
            power = power_rows[source]
            for toward_first in (True, False):
                far = (seconds if toward_first else firsts)[source]
                far_swapped = swapped(far)
                direct = far * fit
                crossed = far_swapped * fit
                if toward_first:
                    numer = jnp.where(is_real, direct - from_later(direct), crossed + from_earlier(crossed))
                else:
                    numer = jnp.where(is_real, direct + from_later(direct), from_earlier(crossed) - crossed)
                denom = (far * far + far_swapped * far_swapped) * power
                high, low = split_two(jnp.concatenate([numer, denom], axis=0))
                columns.append(jnp.concatenate([high, low], axis=0))
        received = lax.dot_general(
            jnp.concatenate(columns, axis=1), onehot[...], (((1,), (1,)), ((), ())), preferred_element_type=F32)
        received = received[0:16] + received[16:32]
        solved = (received[0:8] * weight_rows) / jnp.maximum(received[8:16] * weight_rows, 1.0)
        blended = 0.5 * gains_now + 0.5 * to_halves(solved)
        packed = weight_halves * blended

        width = 384 if turn == 0 else 256
        for z in range(2):
            mixed[turn, 2 * x + z, :, 0:256] = packed[z * 8:z * 8 + 8]
            if turn == 0:
                mixed[turn, 2 * x + z, :, 256:384] = weight_halves[z * 8:z * 8 + 8, 0:LANES]

        def planes(first, count):
            return mixed.at[turn, pl.ds(first, count), :, pl.ds(0, width)]

        line_copies, far_copies = [], []
        for other_x in range(LINE):
            up = remote(planes(2 * x + 1, 1), planes(8 + x, 1), s_mix.at[turn, 3 + other_x],
                        r_mix.at[turn, 4 + x], plane(y + 1, other_x))
            down = remote(planes(2 * x, 1), planes(12 + x, 1), s_mix.at[turn, 7 + other_x],
                          r_mix.at[turn, 8 + x], plane(y - 1, other_x))
            far_copies.append((jnp.logical_and(above, other_x <= x), up))
            far_copies.append((jnp.logical_and(below, other_x >= x), down))
        for needed, copy in far_copies:
            pl.when(needed)(copy.start)
        for step in (2, 1, 3):
            copy = remote(planes(2 * x, 2), planes(2 * x, 2), s_mix.at[turn, step - 1], r_mix.at[turn, x],
                          plane(y, lax.rem(x + step, LINE)))
            copy.start()
            line_copies.append(copy)

        for step in range(1, LINE):
            source_x = lax.rem(x + step, LINE)
            remote(planes(2 * source_x, 2), planes(2 * source_x, 2), s_mix.at[turn, step - 1],
                   r_mix.at[turn, source_x], plane(y, source_x)).wait_recv()
        for source_x in range(LINE):
            from_above = remote(planes(12 + source_x, 1), planes(12 + source_x, 1), s_mix.at[turn, 3 + source_x],
                                r_mix.at[turn, 8 + source_x], plane(y + 1, source_x))
            from_below = remote(planes(8 + source_x, 1), planes(8 + source_x, 1), s_mix.at[turn, 7 + source_x],
                                r_mix.at[turn, 4 + source_x], plane(y - 1, source_x))
            pl.when(jnp.logical_and(above, source_x <= x))(from_above.wait_recv)
            pl.when(jnp.logical_and(below, source_x >= x))(from_below.wait_recv)
        high, low = split_two(mixed[turn, :, :, 0:width].reshape(128, width))
        summed = jnp.dot(smoothing_both, high, preferred_element_type=F32)
        summed = summed[0:16] + summed[16:32] + jnp.dot(smoothing_high, low, preferred_element_type=F32)
        if turn == 0:
            inverse = 1.0 / jnp.maximum(summed[:, 256:384], 1.0)
            inverse = jnp.concatenate([inverse, inverse], axis=1)
        gains_now = summed[:, 0:256] * inverse

        if turn == ITERS - 1:
            for z in range(2):
                for channel in range(2):
                    for row in range(8):
                        half, lane, part = row // 4, (row // 2) % 2, row % 2
                        at = z * 8 + half * 4 + part * 2 + channel
                        stage[z, channel, row:row + 1, :] = gains_now[at:at + 1, lane * LANES:(lane + 1) * LANES]
            gain_copies = []
            for step in FAR_FIRST:
                other, device = ring(step)
                copy = remote(stage.at[lax.div(other, BL)], gains_out.at[:, me], s_gain.at[step], r_gain.at[step], device)
                copy.start()
                gain_copies.append(copy)
            sends.extend(gain_copies)
            gains_out[:, me] = stage[z_hi]

        put_ends(gains_now)
        for source in range(BL):
            near, far = firsts[source], seconds[source]
            direct = near * far
            crossed = near * swapped(far)
            joint = jnp.where(is_real, direct + from_later(direct), crossed - from_earlier(crossed))
            joint_out[turn, source] = joint[0:4]
            joint_out[turn, BL + source] = joint[4:8]
        joint_copies = to_ring(joint_out.at[turn], joint_in.at[turn + 1], s_joint.at[turn], r_joint.at[turn])

        for copy in line_copies:
            copy.wait_send()
        for needed, copy in far_copies:
            pl.when(needed)(copy.wait_send)

    for copy in joint_copies:
        copy.wait_recv()
    for channel in range(2):
        totals = corrupted(joint_in.at[ITERS], channel)
        for part in range(2):
            residual_out[pl.ds(channel * 32 + part, TIMES, stride=2), :] = observed[channel, part] - totals[part]
    for copy in gain_copies:
        copy.wait_recv()
    for copy in sends:
        copy.wait_send()


def local(visibility_noise, baseline_wavelength_coords, station_pair, comp_position, comp_flux,
          comp_spectral, comp_count, true_gains, start_gains, channel_flags):
    vmem = pl.BlockSpec(memory_space=VMEM)
    smem = pl.BlockSpec(memory_space=SMEM)
    anywhere = pl.BlockSpec(memory_space=pltpu.MemorySpace.HBM)
    dma = pltpu.SemaphoreType.DMA
    def tiles(gains):
        return gains.reshape(2, DIRS, 2, 4, LANES).transpose(0, 1, 3, 2, 4).reshape(2 * DIRS * 8, LANES)

    gains, residual = pl.pallas_call(
        calibrate_kernel,
        out_shape=(pltpu.VMEM((2, DIRS, 8, LANES), F32), pltpu.VMEM((64, LANES), F32)),
        in_specs=[anywhere, anywhere, vmem, vmem, vmem, vmem, smem, anywhere, anywhere, smem],
        out_specs=(vmem, vmem),
        scratch_shapes=[
            pltpu.VMEM((64, LANES), F32),
            pltpu.VMEM((3, TIMES, LANES), F32),
            pltpu.VMEM((256, LANES), F32),
            pltpu.VMEM((256, LANES), F32),
            pltpu.VMEM((BL, 8, LANES), F32),
            pltpu.VMEM((BL, 8, LANES), jnp.int32),
            pltpu.SMEM((BL, 8, LANES), F32),
            pltpu.SMEM((BL, 8, LANES), jnp.int32),
            pltpu.VMEM((COMPONENTS, 4, TIMES, LANES), F32),
            pltpu.VMEM((2, DIRS, 2, TIMES, LANES), F32),
            pltpu.VMEM((STATIONS, 2 * LANES), BF16),
            pltpu.VMEM((STATIONS, BL * 2 * LANES), BF16),
            pltpu.VMEM((2, 2, TIMES, LANES), F32),
            pltpu.VMEM((DIRS, 4, LANES), F32),
            pltpu.VMEM((BL, 8, LANES), F32),
            pltpu.VMEM((BL, 8, LANES), F32),
            pltpu.VMEM((2, 8, 256), F32),
            pltpu.VMEM((2, 8, LANES), F32),
            pltpu.VMEM((2, 8, LANES), F32),
            pltpu.VMEM((RING, 8, LANES), F32),
            pltpu.VMEM((RING, 8, LANES), F32),
            pltpu.VMEM((ITERS, RING, 4, LANES), F32),
            pltpu.VMEM((ITERS, RING, 4, LANES), F32),
            pltpu.VMEM((ITERS, RING, 4, LANES), F32),
            pltpu.VMEM((ITERS + 1, RING, 4, LANES), F32),
            pltpu.VMEM((ITERS, 16, 8, 384), F32),
            pltpu.VMEM((2, 2, 8, LANES), F32),
            dma((6,)), dma((BL,)), dma((BL,)), dma((BL,)), dma((BL,)),
            dma(()), dma(()),
            dma((RING,)), dma((RING,)),
            dma((ITERS, RING)), dma((ITERS, RING)),
            dma((ITERS, RING)), dma((ITERS, RING)),
            dma((ITERS, 11)), dma((ITERS, 12)),
            dma((RING,)), dma((RING,)),
        ],
        compiler_params=pltpu.CompilerParams(
            collective_id=0, has_side_effects=True, vmem_limit_bytes=56 * 1024 * 1024),
        name="calibrate",
    )(visibility_noise.reshape(64, LANES), baseline_wavelength_coords, station_pair, comp_position, comp_flux,
      comp_spectral, comp_count, tiles(true_gains), tiles(start_gains), channel_flags)
    gains = gains.reshape(2, DIRS, 4, 2, LANES).transpose(0, 1, 3, 2, 4).reshape(2, DIRS, 2, STATIONS)
    return gains, residual.reshape(2, TIMES, 2, LANES)


def solution(mesh):
    in_specs = (
        P("freq", None, None, "bl"),
        P(None, None, "bl"),
        P(None, "bl"),
        P("bl", None, None),
        P("bl", None),
        P("bl", None),
        P("bl"),
        P("freq", None, None, None),
        P("freq", None, None, None),
        P("freq"),
    )
    out_specs = (P("freq", None, None, None), P("freq", None, None, "bl"))
    return jax.shard_map(local, mesh=mesh, in_specs=in_specs, out_specs=out_specs, check_vma=False)
```

```python
import jax
import jax.numpy as jnp
from jax import lax
from jax.experimental import pallas as pl
from jax.experimental.pallas import tpu as pltpu
from jax.sharding import PartitionSpec as P

F32 = jnp.float32
BF16 = jnp.bfloat16
MESH = pl.DeviceIdType.MESH
VMEM = pltpu.MemorySpace.VMEM
SMEM = pltpu.MemorySpace.SMEM

NEAR = (1, 15, 2, 14, 3, 13, 4, 12, 0)
FAR = (8, 7, 9, 6, 10, 5, 11)
BL = 8
LINE = 4
RING = 16
ITERS = 3
DIRS = 16
TIMES = 16
STATIONS = 512
COMPONENTS = 512
LANES = 128
REACH = 8.0
SPREAD = 4.0

SIN_SCALE, SIN_FACTORS = -0.5546349618, (-0.978320908350836, -3.6046909402902565, 5.789750187942454)
COS_SCALE, COS_FACTORS = -1.2221263189, (-0.24999786765951873, -3.0567664626737323, 3.2729900649797434)


def factored(factors, at):
    return (at + factors[0]) * (at * (at + factors[1]) + factors[2])


def split_two(value):
    high = value.astype(BF16)
    low = (value - high.astype(F32)).astype(BF16)
    return high, low


def ratio_of(channel):
    return 0.5 + (channel.astype(F32) + 0.5) / 128.0


def calibrate_kernel(noise_hbm, coords_hbm, pair, position, flux, spectral, count, true_hbm, start_hbm, flags,
                     gains_out, residual_out,
                     noise, coords, true_gains, start_gains, params, ids, params_scalar, ids_scalar, running, model,
                     own_onehot, onehot, observed, joint_true, firsts, seconds, owned, first_out, first_in,
                     energy, energy_in, joint_start,
                     fits_0, fits_1, fits_2, fits_3, fits_in_0, fits_in_1, fits_in_2, fits_in_3,
                     joint_out_0, joint_out_1, joint_out_2, joint_out_3, joint_in_0, joint_in_1, joint_in_2, joint_in_3,
                     mixed, stage,
                     s_load, s_param, r_param, s_ids, r_ids,
                     s_first, r_first, s_energy, r_energy, s_fit, r_fit, s_joint, r_joint,
                     s_mix, r_mix, s_gain, r_gain):
    freq = lax.axis_index("freq")
    bl = lax.axis_index("bl")
    y = lax.div(freq, 8)
    z_hi = lax.rem(lax.div(freq, LINE), 2)
    x = lax.rem(freq, LINE)
    me = z_hi * BL + bl
    above, below = y < lax.axis_size("freq") // 8 - 1, y > 0

    z_lo, core = lax.div(bl, 2), lax.rem(bl, 2)
    fits = (fits_0, fits_1, fits_2, fits_3)
    fits_in = (fits_in_0, fits_in_1, fits_in_2, fits_in_3)
    joint_out = (joint_out_0, joint_out_1, joint_out_2, joint_out_3)
    joint_in = (joint_in_0, joint_in_1, joint_in_2, joint_in_3)
    places = ((0, 0), (0, 1), (1, 0), (1, 1))

    def ring_device(other):
        return {"freq": (y * 2 + lax.div(other, BL)) * LINE + x, "bl": lax.rem(other, BL)}

    def ring(step):
        other = lax.rem(me + step, RING)
        return other, ring_device(other)

    def plane(other_y, other_x):
        return {"freq": (other_y * 2 + z_hi) * LINE + other_x, "bl": bl}

    loads = []
    for index, (source, target) in enumerate((
            (true_hbm, true_gains), (start_hbm, start_gains), (noise_hbm, noise), (coords_hbm, coords))):
        copy = pltpu.make_async_copy(source, target, s_load.at[index])
        copy.start()
        loads.append(copy)

    mixed[...] = jnp.zeros(mixed.shape, F32)

    barrier = pltpu.get_barrier_semaphore()
    for step in range(1, RING):
        pl.semaphore_signal(barrier, inc=1, device_id=ring(step)[1], device_id_type=MESH)
    for step in range(1, LINE):
        pl.semaphore_signal(barrier, inc=1, device_id=plane(y, lax.rem(x + step, LINE)), device_id_type=MESH)

    @pl.when(above)
    def _():
        for other_x in range(LINE):
            pl.semaphore_signal(barrier, inc=1, device_id=plane(y + 1, other_x), device_id_type=MESH)

    @pl.when(below)
    def _():
        for other_x in range(LINE):
            pl.semaphore_signal(barrier, inc=1, device_id=plane(y - 1, other_x), device_id_type=MESH)

    def both(values):
        return jnp.concatenate([values[0:1], values[1:2]], axis=1)

    l, m = both(position[:, 0, :]), both(position[:, 1, :])
    square = l * l + m * m
    params[bl, 0:1, :] = l
    params[bl, 1:2, :] = m
    params[bl, 2:3, :] = -square / (1.0 + jnp.sqrt(1.0 - square))
    lane = lax.broadcasted_iota(jnp.int32, (1, LANES), 1)
    lives = jnp.where(lane < 64, count[0], count[1])
    fluxes = jnp.where((lane & 63) < lives, both(flux[...]), 0.0)
    index = both(spectral[...])
    extra = jnp.zeros((1, LANES), F32)
    for channel in range(2):
        ratio = jnp.full((1, LANES), 1.0, F32) * ratio_of(freq * 2 + channel)
        spectrum = fluxes * jnp.exp(index * jnp.log(ratio))
        params[bl, 3 + channel:4 + channel, :] = spectrum
        for half in range(2):
            total = jnp.sum(jnp.where((lane >> 6) == half, spectrum, 0.0), axis=1, keepdims=True)
            extra = jnp.where(lane == half * 2 + channel, total, extra)
    params[bl, 5:6, :] = extra
    ids[bl, 0:2, :] = pair[...]
    ids[bl, 2:3, :] = jnp.where(lane == 0, count[0], count[1])

    station = lax.broadcasted_iota(jnp.int32, (STATIONS, LANES), 0)
    for end in range(2):
        own_onehot[:, end * LANES:(end + 1) * LANES] = jnp.where(station == pair[end:end + 1, :], 1.0, 0.0).astype(BF16)
    for copy in loads:
        copy.wait()

    def local_joint(gains):
        rows = []
        for part in range(2):
            rows.append(jnp.concatenate(
                [gains[pl.ds(tile * 2 + part, 32, stride=8), :] for tile in range(4)], axis=1))
        high, low = split_two(jnp.concatenate(rows, axis=0))
        ends = jnp.dot(jnp.concatenate([high, low], axis=0), own_onehot[...], preferred_element_type=F32)
        ends = ends[0:64] + ends[64:128]
        pr, pi = ends[0:32, 0:LANES], ends[32:64, 0:LANES]
        qr, qi = ends[0:32, LANES:], ends[32:64, LANES:]
        return pr * qr + pi * qi, pi * qr - pr * qi

    for ref, gains in ((joint_true, true_gains), (joint_start, start_gains)):
        parts = local_joint(gains)
        for channel in range(2):
            for part in range(2):
                for patch in range(DIRS):
                    at = channel * DIRS + patch
                    offset = lax.rem((patch % BL) // 2 + LINE - z_lo, LINE)
                    slot = (patch // BL) * 2 + patch % 2
                    ref[offset, slot, part * 2 + channel:part * 2 + channel + 1, :] = parts[part][at:at + 1]

    away = (1 - z_hi) * BL + bl
    for channel in range(2):
        first_out[channel] = start_gains[pl.ds(pl.multiple_of(channel * 128 + away * 8, 8), 8), :]

    neighbours = jnp.where(above, LINE, 0) + jnp.where(below, LINE, 0)
    pl.semaphore_wait(barrier, RING - 1 + LINE - 1 + neighbours)

    sends = []

    def remote(src, dst, send, recv, device):
        return pltpu.make_async_remote_copy(
            src_ref=src, dst_ref=dst, send_sem=send, recv_sem=recv, device_id=device, device_id_type=MESH)

    param_copies = []
    for step in (4, 3, 5, 2, 6, 1, 7):
        device = {"bl": lax.rem(bl + step, BL)}
        for outgoing, send, recv in ((params, s_param, r_param), (ids, s_ids, r_ids)):
            copy = remote(outgoing.at[bl], outgoing.at[bl], send.at[step], recv.at[step], device)
            copy.start()
            param_copies.append(copy)
    sends.extend(param_copies)
    first_copy = remote(first_out, first_in, s_first, r_first, ring(BL)[1])
    first_copy.start()
    sends.append(first_copy)
    for copy in param_copies:
        copy.wait_recv()
    scalars = [pltpu.make_async_copy(params, params_scalar, s_load.at[4]),
               pltpu.make_async_copy(ids, ids_scalar, s_load.at[5])]
    for copy in scalars:
        copy.start()
    for copy in scalars:
        copy.wait()

    ratio_zero, ratio_one = ratio_of(freq * 2), ratio_of(freq * 2 + 1)
    relative = ratio_one / ratio_zero
    u, v, w = coords[0] * ratio_zero, coords[1] * ratio_zero, coords[2] * ratio_zero

    def lives_of(patch):
        return ids_scalar[patch >> 1, 2, patch & 1]

    def one_component(component, state):
        sums, (patch, slot, live) = list(state[0:4]), state[4:7]
        device, column = patch >> 1, (patch & 1) * 64 + slot
        delay = (u * params_scalar[device, 0, column] + v * params_scalar[device, 1, column]
                 + w * params_scalar[device, 2, column])
        keep = jnp.where(slot == 0, 0.0, 1.0)
        for channel, turns in enumerate((delay, delay * relative)):
            turns = turns - jnp.round(turns)
            square = turns * turns
            sine = turns * factored(SIN_FACTORS, square)
            scaled = sine * params_scalar[device, 3 + channel, column]
            sums[2 * channel] = sums[2 * channel] * keep + scaled * sine
            sums[2 * channel + 1] = sums[2 * channel + 1] * keep + scaled * factored(COS_FACTORS, square)
        for place in range(4):
            running[component, place] = sums[place]
        done = slot + 1 >= live
        patch = jnp.minimum(patch + jnp.where(done, 1, 0), DIRS - 1)
        slot = jnp.where(done, 0, slot + 1)
        return (*sums, patch, slot, lives_of(patch))

    zero = jnp.zeros((TIMES, LANES), F32)
    start = jnp.int32(0)
    lax.fori_loop(0, COMPONENTS, one_component, (zero,) * 4 + (start, start, lives_of(start)), unroll=16)

    def finish_patch(patch, end):
        end = end + lives_of(patch)
        last = jnp.clip(end - 1, 0, COMPONENTS - 1)
        for channel in range(2):
            total = params_scalar[patch >> 1, 5, (patch & 1) * 2 + channel]
            model[channel, patch, 0] = total - (2.0 * SIN_SCALE * SIN_SCALE) * running[last, 2 * channel]
            model[channel, patch, 1] = (-2.0 * SIN_SCALE * COS_SCALE) * running[last, 2 * channel + 1]
        return end

    lax.fori_loop(0, DIRS, finish_patch, start, unroll=True)

    def chip_of(offset):
        return lax.rem(z_lo + offset, LINE)

    def corrupted(row, wait=None):
        totals = [jnp.zeros((TIMES, LANES), F32) for _ in range(4)]
        for offset in (2, 1, 3, 0):
            if wait is not None:
                wait(offset)
            for slot, (z, which) in enumerate(places):
                patch = z * BL + chip_of(offset) * 2 + which
                for channel in range(2):
                    jr, ji = row(offset, slot, channel), row(offset, slot, 2 + channel)
                    mr, mi = model[channel, patch, 0], model[channel, patch, 1]
                    totals[2 * channel] += jr * mr - ji * mi
                    totals[2 * channel + 1] += jr * mi + ji * mr
        return totals

    def row_at_start(ref):
        return lambda offset, slot, at: ref[offset, slot, at:at + 1, :]

    def row_at(round_index):
        if round_index == 0:
            return row_at_start(joint_start)
        return lambda offset, slot, at: joint_in[offset][round_index - 1, slot, at:at + 1, :]

    totals = corrupted(row_at_start(joint_true))
    for channel in range(2):
        for part in range(2):
            observed[channel, part] = noise[pl.ds(channel * 32 + part, TIMES, stride=2), :] + totals[2 * channel + part]

    def put_energy(patch, _):
        for channel in range(2):
            mr, mi = model[channel, patch, 0], model[channel, patch, 1]
            row = jnp.sum(mr * mr + mi * mi, axis=0, keepdims=True)
            weight = jnp.full((1, LANES), 1.0, F32) * (1.0 - flags[channel].astype(F32))
            for part in range(2):
                at = part * 2 + channel
                energy[patch, at:at + 1, :] = row
                energy[patch, 4 + at:5 + at, :] = weight
        return 0

    lax.fori_loop(0, DIRS, put_energy, 0, unroll=True)

    def ring_copy(src, dst, send, recv, other):
        return remote(src, dst, send.at[other], recv.at[me], ring_device(other))

    def send_ring(src, dst, send, recv, other):
        copy = ring_copy(src, dst, send, recv, other)
        copy.start()
        sends.append(copy)

    def wait_ring(landing, send, recv, other):
        remote(landing, landing, send.at[other], recv.at[other], ring_device(other)).wait_recv()

    def others_of(offset):
        some = ((1 - z_hi, 0), (1 - z_hi, 1), (z_hi, 1 - core)) if offset == 0 else places
        return [(z * 2 + which, z * BL + chip_of(offset) * 2 + which) for z, which in some]

    own_slot = z_hi * 2 + core

    def send_offset(outgoing, incoming, send, recv, turn, offset):
        back = (LINE - offset) % LINE
        for slot, other in others_of(offset):
            copy = remote(outgoing[offset].at[turn, slot], incoming[back].at[turn, own_slot],
                          send.at[turn, offset * 4 + slot], recv.at[turn, back * 4 + own_slot], ring_device(other))
            copy.start()
            sends.append(copy)
        if offset == 0:
            incoming[0][turn, own_slot] = outgoing[0][turn, own_slot]

    def wait_offset(incoming, send, recv, turn, offset):
        for slot, other in others_of(offset):
            landed = incoming[offset].at[turn, slot]
            remote(landed, landed, send.at[turn, offset * 4 + slot], recv.at[turn, offset * 4 + slot],
                   ring_device(other)).wait_recv()

    for step in FAR + NEAR[:-1]:
        other = ring(step)[0]
        send_ring(energy.at[other], energy_in.at[me], s_energy, r_energy, other)
    energy_in[me] = energy[me]

    row8 = lax.broadcasted_iota(jnp.int32, (8, LANES), 0)
    is_real = (row8 & 2) == 0

    def from_later(value):
        return pltpu.roll(value, 6, 0)

    def from_earlier(value):
        return pltpu.roll(value, 2, 0)

    def swapped(value):
        return jnp.where(is_real, from_later(value), from_earlier(value))

    def split_rows(gains):
        return jnp.concatenate(split_two(jnp.concatenate([
            jnp.concatenate([gains[0:4], gains[8:12]], axis=0),
            jnp.concatenate([gains[4:8], gains[12:16]], axis=0)], axis=1)), axis=0)

    def put_ends(rows, chip):
        columns = onehot[:, pl.ds(pl.multiple_of(chip * 512, 512), 512)]
        both = jnp.dot(rows, columns, preferred_element_type=F32)
        both = both[0:8] + both[8:16]
        pairs = []
        for which in range(2):
            start = which * 2 * LANES
            near, far = both[:, start:start + LANES], both[:, start + LANES:start + 2 * LANES]
            firsts[chip * 2 + which] = near
            seconds[chip * 2 + which] = far
            pairs.append((near, far))
        return pairs

    def to_halves(rows):
        return jnp.concatenate([
            rows[0:4, 0:256], rows[0:4, 256:512], rows[4:8, 0:256], rows[4:8, 256:512]], axis=0)

    here = lax.broadcasted_iota(jnp.int32, (16, 128), 0)
    there = lax.broadcasted_iota(jnp.int32, (16, 128), 1)
    slot = there >> 3
    slot_y = jnp.where(slot < 8, 0, jnp.where(slot < 12, 1, -1))
    slot_z = jnp.where(slot < 8, slot & 1, jnp.where(slot < 12, 1, 0))
    slot_x = jnp.where(slot < 8, slot >> 1, slot & 3)
    apart = (16 * slot_y + 8 * ((here >> 3) - slot_z) + 2 * (x - slot_x) + (here & 1) - (there & 1)).astype(F32)
    reached = jnp.where((here & 6) == (there & 6), jnp.where(jnp.abs(apart) <= REACH, 1.0, 0.0), 0.0)
    smoothing = jnp.exp(-(apart * apart) / (2.0 * SPREAD * SPREAD)) * reached

    smoothing_high, smoothing_low = split_two(smoothing)
    smoothing_both = jnp.concatenate([smoothing_high, smoothing_low], axis=0)

    def wait_joint(round_index):
        if round_index == 0:
            return None
        return lambda offset: wait_offset(joint_in, s_joint, r_joint, round_index - 1, offset)

    def fit_and_send(turn):
        row = row_at(turn)
        totals = corrupted(row, wait_joint(turn))
        rests = [observed[place // 2, place % 2] - totals[place] for place in range(4)]
        for offset in (0, 1, 3, 2):
            for slot, (z, which) in enumerate(places):
                patch = z * BL + chip_of(offset) * 2 + which
                for channel in range(2):
                    rest_r, rest_i = rests[2 * channel], rests[2 * channel + 1]
                    mr, mi = model[channel, patch, 0], model[channel, patch, 1]
                    power = energy[patch, channel:channel + 1, :]
                    for part, value in enumerate((mr * rest_r + mi * rest_i, mr * rest_i - mi * rest_r)):
                        at = part * 2 + channel
                        fits[offset][turn, slot, at:at + 1, :] = (
                            jnp.sum(value, axis=0, keepdims=True) + row(offset, slot, at) * power)
            send_offset(fits, fits_in, s_fit, r_fit, turn, offset)

    inverse = None
    weight_halves = None
    weight_rows = None
    for turn in range(ITERS):
        fit_and_send(turn)
        if turn == 0:
            for source in range(BL):
                for end in range(2):
                    row = ids[source, end:end + 1, :]
                    start = (source * 2 + end) * LANES
                    onehot[:, start:start + LANES] = jnp.where(station == row, 1.0, 0.0).astype(BF16)
            first_copy.wait_recv()
            for channel in range(2):
                own = start_gains[pl.ds(pl.multiple_of(channel * 128 + me * 8, 8), 8), :]
                other = first_in[channel]
                for row in range(8):
                    half, lane, part = row // 4, (row // 2) % 2, row % 2
                    at = half * 4 + part * 2 + channel
                    owned[z_hi, at:at + 1, lane * LANES:(lane + 1) * LANES] = own[row:row + 1]
                    owned[1 - z_hi, at:at + 1, lane * LANES:(lane + 1) * LANES] = other[row:row + 1]
            gains_now = owned[...].reshape(16, 256)
            rows = split_rows(gains_now)
            for chip in range(LINE):
                put_ends(rows, chip)
            for step in NEAR[:-1] + FAR:
                other = ring(step)[0]
                wait_ring(energy_in.at[other], s_energy, r_energy, other)
            weight_rows = jnp.concatenate([energy_in[0, 4:8], energy_in[BL, 4:8]], axis=0)
            weight_rows = jnp.concatenate([weight_rows] * 4, axis=1)
            weight_halves = to_halves(weight_rows)

        received = jnp.zeros((32, STATIONS), F32)
        for offset in (2, 1, 3, 0):
            chip = chip_of(offset)
            wait_offset(fits_in, s_fit, r_fit, turn, offset)
            columns = []
            for which in range(2):
                source = chip * 2 + which
                fit = jnp.concatenate([fits_in[offset][turn, which], fits_in[offset][turn, 2 + which]], axis=0)
                power = jnp.concatenate([energy_in[source, 0:4], energy_in[BL + source, 0:4]], axis=0)
                for toward_first in (True, False):
                    far = (seconds if toward_first else firsts)[source]
                    far_swapped = swapped(far)
                    direct = far * fit
                    crossed = far_swapped * fit
                    if toward_first:
                        numer = jnp.where(is_real, direct - from_later(direct), crossed + from_earlier(crossed))
                    else:
                        numer = jnp.where(is_real, direct + from_later(direct), from_earlier(crossed) - crossed)
                    denom = (far * far + far_swapped * far_swapped) * power
                    columns.append(jnp.concatenate(split_two(jnp.concatenate([numer, denom], axis=0)), axis=0))
            received = received + lax.dot_general(
                jnp.concatenate(columns, axis=1), onehot[:, pl.ds(pl.multiple_of(chip * 512, 512), 512)],
                (((1,), (1,)), ((), ())), preferred_element_type=F32)
        received = received[0:16] + received[16:32]
        solved = (received[0:8] * weight_rows) / jnp.maximum(received[8:16] * weight_rows, 1.0)
        blended = 0.5 * gains_now + 0.5 * to_halves(solved)
        packed = weight_halves * blended

        width = 384 if turn == 0 else 256
        for z in range(2):
            mixed[turn, 2 * x + z, :, 0:256] = packed[z * 8:z * 8 + 8]
            if turn == 0:
                mixed[turn, 2 * x + z, :, 256:384] = weight_halves[z * 8:z * 8 + 8, 0:LANES]

        def planes(first, count):
            return mixed.at[turn, pl.ds(first, count), :, pl.ds(0, width)]

        line_copies, far_copies = [], []
        for other_x in range(LINE):
            up = remote(planes(2 * x + 1, 1), planes(8 + x, 1), s_mix.at[turn, 3 + other_x],
                        r_mix.at[turn, 4 + x], plane(y + 1, other_x))
            down = remote(planes(2 * x, 1), planes(12 + x, 1), s_mix.at[turn, 7 + other_x],
                          r_mix.at[turn, 8 + x], plane(y - 1, other_x))
            far_copies.append((jnp.logical_and(above, other_x <= x), up))
            far_copies.append((jnp.logical_and(below, other_x >= x), down))
        for needed, copy in far_copies:
            pl.when(needed)(copy.start)
        for step in (2, 1, 3):
            copy = remote(planes(2 * x, 2), planes(2 * x, 2), s_mix.at[turn, step - 1], r_mix.at[turn, x],
                          plane(y, lax.rem(x + step, LINE)))
            copy.start()
            line_copies.append(copy)

        for step in range(1, LINE):
            source_x = lax.rem(x + step, LINE)
            remote(planes(2 * source_x, 2), planes(2 * source_x, 2), s_mix.at[turn, step - 1],
                   r_mix.at[turn, source_x], plane(y, source_x)).wait_recv()
        for source_x in range(LINE):
            from_above = remote(planes(12 + source_x, 1), planes(12 + source_x, 1), s_mix.at[turn, 3 + source_x],
                                r_mix.at[turn, 8 + source_x], plane(y + 1, source_x))
            from_below = remote(planes(8 + source_x, 1), planes(8 + source_x, 1), s_mix.at[turn, 7 + source_x],
                                r_mix.at[turn, 4 + source_x], plane(y - 1, source_x))
            pl.when(jnp.logical_and(above, source_x <= x))(from_above.wait_recv)
            pl.when(jnp.logical_and(below, source_x >= x))(from_below.wait_recv)
        high, low = split_two(mixed[turn, :, :, 0:width].reshape(128, width))
        summed = jnp.dot(smoothing_both, high, preferred_element_type=F32)
        summed = summed[0:16] + summed[16:32] + jnp.dot(smoothing_high, low, preferred_element_type=F32)
        if turn == 0:
            inverse = 1.0 / jnp.maximum(summed[:, 256:384], 1.0)
            inverse = jnp.concatenate([inverse, inverse], axis=1)
        gains_now = summed[:, 0:256] * inverse

        if turn == ITERS - 1:
            for z in range(2):
                for channel in range(2):
                    for row in range(8):
                        half, lane, part = row // 4, (row // 2) % 2, row % 2
                        at = z * 8 + half * 4 + part * 2 + channel
                        stage[z, channel, row:row + 1, :] = gains_now[at:at + 1, lane * LANES:(lane + 1) * LANES]
            for step in FAR + NEAR[:-1]:
                other = ring(step)[0]
                send_ring(stage.at[lax.div(other, BL)], gains_out.at[:, me], s_gain, r_gain, other)
            gains_out[:, me] = stage[z_hi]

        rows = split_rows(gains_now)
        for offset in (0, 1, 3, 2):
            chip = chip_of(offset)
            for which, (near, far) in enumerate(put_ends(rows, chip)):
                direct = near * far
                crossed = near * swapped(far)
                joint = jnp.where(is_real, direct + from_later(direct), crossed - from_earlier(crossed))
                joint_out[offset][turn, which] = joint[0:4]
                joint_out[offset][turn, 2 + which] = joint[4:8]
            send_offset(joint_out, joint_in, s_joint, r_joint, turn, offset)

        for copy in line_copies:
            copy.wait_send()
        for needed, copy in far_copies:
            pl.when(needed)(copy.wait_send)

    totals = corrupted(row_at(ITERS), wait_joint(ITERS))
    for channel in range(2):
        for part in range(2):
            residual_out[pl.ds(channel * 32 + part, TIMES, stride=2), :] = (
                observed[channel, part] - totals[2 * channel + part])
    for step in NEAR[:-1] + FAR:
        other = ring(step)[0]
        wait_ring(gains_out.at[:, other], s_gain, r_gain, other)
    for copy in sends:
        copy.wait_send()


def local(visibility_noise, baseline_wavelength_coords, station_pair, comp_position, comp_flux,
          comp_spectral, comp_count, true_gains, start_gains, channel_flags):
    vmem = pl.BlockSpec(memory_space=VMEM)
    smem = pl.BlockSpec(memory_space=SMEM)
    anywhere = pl.BlockSpec(memory_space=pltpu.MemorySpace.HBM)
    dma = pltpu.SemaphoreType.DMA
    def tiles(gains):
        return gains.reshape(2, DIRS, 2, 4, LANES).transpose(0, 1, 3, 2, 4).reshape(2 * DIRS * 8, LANES)

    gains, residual = pl.pallas_call(
        calibrate_kernel,
        out_shape=(pltpu.VMEM((2, DIRS, 8, LANES), F32), pltpu.VMEM((64, LANES), F32)),
        in_specs=[anywhere, anywhere, vmem, vmem, vmem, vmem, smem, anywhere, anywhere, smem],
        out_specs=(vmem, vmem),
        scratch_shapes=[
            pltpu.VMEM((64, LANES), F32),
            pltpu.VMEM((3, TIMES, LANES), F32),
            pltpu.VMEM((256, LANES), F32),
            pltpu.VMEM((256, LANES), F32),
            pltpu.VMEM((BL, 8, LANES), F32),
            pltpu.VMEM((BL, 8, LANES), jnp.int32),
            pltpu.SMEM((BL, 8, LANES), F32),
            pltpu.SMEM((BL, 8, LANES), jnp.int32),
            pltpu.VMEM((COMPONENTS, 4, TIMES, LANES), F32),
            pltpu.VMEM((2, DIRS, 2, TIMES, LANES), F32),
            pltpu.VMEM((STATIONS, 2 * LANES), BF16),
            pltpu.VMEM((STATIONS, BL * 2 * LANES), BF16),
            pltpu.VMEM((2, 2, TIMES, LANES), F32),
            pltpu.VMEM((LINE, 4, 4, LANES), F32),
            pltpu.VMEM((BL, 8, LANES), F32),
            pltpu.VMEM((BL, 8, LANES), F32),
            pltpu.VMEM((2, 8, 256), F32),
            pltpu.VMEM((2, 8, LANES), F32),
            pltpu.VMEM((2, 8, LANES), F32),
            pltpu.VMEM((RING, 8, LANES), F32),
            pltpu.VMEM((RING, 8, LANES), F32),
            pltpu.VMEM((LINE, 4, 4, LANES), F32),
        ] + [pltpu.VMEM((ITERS, 4, 4, LANES), F32)] * 16 + [
            pltpu.VMEM((ITERS, 16, 8, 384), F32),
            pltpu.VMEM((2, 2, 8, LANES), F32),
            dma((6,)), dma((BL,)), dma((BL,)), dma((BL,)), dma((BL,)),
            dma(()), dma(()),
            dma((RING,)), dma((RING,)),
            dma((ITERS, RING)), dma((ITERS, RING)),
            dma((ITERS, RING)), dma((ITERS, RING)),
            dma((ITERS, 11)), dma((ITERS, 12)),
            dma((RING,)), dma((RING,)),
        ],
        compiler_params=pltpu.CompilerParams(
            collective_id=0, has_side_effects=True, vmem_limit_bytes=56 * 1024 * 1024),
        name="calibrate",
    )(visibility_noise.reshape(64, LANES), baseline_wavelength_coords, station_pair, comp_position, comp_flux,
      comp_spectral, comp_count, tiles(true_gains), tiles(start_gains), channel_flags)
    gains = gains.reshape(2, DIRS, 4, 2, LANES).transpose(0, 1, 3, 2, 4).reshape(2, DIRS, 2, STATIONS)
    return gains, residual.reshape(2, TIMES, 2, LANES)


def solution(mesh):
    in_specs = (
        P("freq", None, None, "bl"),
        P(None, None, "bl"),
        P(None, "bl"),
        P("bl", None, None),
        P("bl", None),
        P("bl", None),
        P("bl"),
        P("freq", None, None, None),
        P("freq", None, None, None),
        P("freq"),
    )
    out_specs = (P("freq", None, None, None), P("freq", None, None, "bl"))
    return jax.shard_map(local, mesh=mesh, in_specs=in_specs, out_specs=out_specs, check_vma=False)
```

```python
import jax
import jax.numpy as jnp
from jax import lax
from jax.experimental import pallas as pl
from jax.experimental.pallas import tpu as pltpu
from jax.sharding import PartitionSpec as P

F32 = jnp.float32
BF16 = jnp.bfloat16
MESH = pl.DeviceIdType.MESH
VMEM = pltpu.MemorySpace.VMEM
SMEM = pltpu.MemorySpace.SMEM

NEAR = (1, 15, 2, 14, 3, 13, 4, 12, 0)
FAR = (8, 7, 9, 6, 10, 5, 11)
BL = 8
LINE = 4
RING = 16
ITERS = 3
DIRS = 16
TIMES = 16
STATIONS = 512
COMPONENTS = 512
LANES = 128
REACH = 8.0
SPREAD = 4.0

SIN_SCALE, SIN_FACTORS = -0.5546349618, (-0.978320908350836, -3.6046909402902565, 5.789750187942454)
COS_SCALE, COS_FACTORS = -1.2221263189, (-0.24999786765951873, -3.0567664626737323, 3.2729900649797434)


def factored(factors, at):
    return (at + factors[0]) * (at * (at + factors[1]) + factors[2])


def split_two(value):
    high = value.astype(BF16)
    low = (value - high.astype(F32)).astype(BF16)
    return high, low


def ratio_of(channel):
    return 0.5 + (channel.astype(F32) + 0.5) / 128.0


def calibrate_kernel(noise_hbm, coords_hbm, pair, position, flux, spectral, count, true_hbm, start_hbm, flags,
                     gains_out, residual_out,
                     noise, coords, true_gains, start_gains, params, ids, counts, params_scalar, counts_scalar, running, model,
                     own_onehot, onehot, observed, joint_true, firsts, seconds, owned, first_out, first_in,
                     energy, energy_in, joint_start,
                     fits_0, fits_1, fits_2, fits_3, fits_in_0, fits_in_1, fits_in_2, fits_in_3,
                     joint_out_0, joint_out_1, joint_out_2, joint_out_3, joint_in_0, joint_in_1, joint_in_2, joint_in_3,
                     mixed, mixed_far, stage,
                     s_load, s_param, r_param, s_ids, r_ids,
                     s_first, r_first, s_energy, r_energy, s_fit, r_fit, s_joint, r_joint,
                     s_mix, r_mix, s_gain, r_gain):
    freq = lax.axis_index("freq")
    bl = lax.axis_index("bl")
    y = lax.div(freq, 8)
    z_hi = lax.rem(lax.div(freq, LINE), 2)
    x = lax.rem(freq, LINE)
    me = z_hi * BL + bl
    above, below = y < lax.axis_size("freq") // 8 - 1, y > 0

    z_lo, core = lax.div(bl, 2), lax.rem(bl, 2)
    fits = (fits_0, fits_1, fits_2, fits_3)
    fits_in = (fits_in_0, fits_in_1, fits_in_2, fits_in_3)
    joint_out = (joint_out_0, joint_out_1, joint_out_2, joint_out_3)
    joint_in = (joint_in_0, joint_in_1, joint_in_2, joint_in_3)
    places = ((0, 0), (0, 1), (1, 0), (1, 1))

    def ring_device(other):
        return {"freq": (y * 2 + lax.div(other, BL)) * LINE + x, "bl": lax.rem(other, BL)}

    def ring(step):
        other = lax.rem(me + step, RING)
        return other, ring_device(other)

    def plane(other_y, other_x):
        return {"freq": (other_y * 2 + z_hi) * LINE + other_x, "bl": bl}

    loads = []
    for index, (source, target) in enumerate((
            (true_hbm, true_gains), (start_hbm, start_gains), (noise_hbm, noise), (coords_hbm, coords))):
        copy = pltpu.make_async_copy(source, target, s_load.at[index])
        copy.start()
        loads.append(copy)

    mixed_far[...] = jnp.zeros(mixed_far.shape, F32)

    barrier = pltpu.get_barrier_semaphore()
    for step in range(1, RING):
        pl.semaphore_signal(barrier, inc=1, device_id=ring(step)[1], device_id_type=MESH)
    for step in range(1, LINE):
        pl.semaphore_signal(barrier, inc=1, device_id=plane(y, lax.rem(x + step, LINE)), device_id_type=MESH)

    @pl.when(above)
    def _():
        for other_x in range(LINE):
            pl.semaphore_signal(barrier, inc=1, device_id=plane(y + 1, other_x), device_id_type=MESH)

    @pl.when(below)
    def _():
        for other_x in range(LINE):
            pl.semaphore_signal(barrier, inc=1, device_id=plane(y - 1, other_x), device_id_type=MESH)

    def both(values):
        return jnp.concatenate([values[0:1], values[1:2]], axis=1)

    l, m = both(position[:, 0, :]), both(position[:, 1, :])
    square = l * l + m * m
    params[bl, 0:1, :] = l
    params[bl, 1:2, :] = m
    params[bl, 2:3, :] = -square / (1.0 + jnp.sqrt(1.0 - square))
    lane = lax.broadcasted_iota(jnp.int32, (1, LANES), 1)
    lives = jnp.where(lane < 64, count[0], count[1])
    fluxes = jnp.where((lane & 63) < lives, both(flux[...]), 0.0)
    index = both(spectral[...])
    extra = jnp.zeros((1, LANES), F32)
    for channel in range(2):
        ratio = jnp.full((1, LANES), 1.0, F32) * ratio_of(freq * 2 + channel)
        spectrum = fluxes * jnp.exp(index * jnp.log(ratio))
        params[bl, 3 + channel:4 + channel, :] = spectrum
        for half in range(2):
            total = jnp.sum(jnp.where((lane >> 6) == half, spectrum, 0.0), axis=1, keepdims=True)
            extra = jnp.where(lane == half * 2 + channel, total, extra)
    params[bl, 5:6, :] = extra
    ids[bl, 0:2, :] = pair[...]
    ids[bl, 2:3, :] = jnp.where(lane == 0, count[0], count[1])

    station = lax.broadcasted_iota(jnp.int32, (STATIONS, LANES), 0)
    for end in range(2):
        own_onehot[:, end * LANES:(end + 1) * LANES] = jnp.where(station == pair[end:end + 1, :], 1.0, 0.0).astype(BF16)
    for copy in loads:
        copy.wait()

    def local_joint(gains):
        rows = []
        for part in range(2):
            rows.append(jnp.concatenate(
                [gains[pl.ds(tile * 2 + part, 32, stride=8), :] for tile in range(4)], axis=1))
        high, low = split_two(jnp.concatenate(rows, axis=0))
        ends = jnp.dot(jnp.concatenate([high, low], axis=0), own_onehot[...], preferred_element_type=F32)
        ends = ends[0:64] + ends[64:128]
        pr, pi = ends[0:32, 0:LANES], ends[32:64, 0:LANES]
        qr, qi = ends[0:32, LANES:], ends[32:64, LANES:]
        return pr * qr + pi * qi, pi * qr - pr * qi

    for ref, gains in ((joint_true, true_gains), (joint_start, start_gains)):
        parts = local_joint(gains)
        for channel in range(2):
            for part in range(2):
                for patch in range(DIRS):
                    at = channel * DIRS + patch
                    offset = lax.rem((patch % BL) // 2 + LINE - z_lo, LINE)
                    slot = (patch // BL) * 2 + patch % 2
                    ref[offset, slot, part * 2 + channel:part * 2 + channel + 1, :] = parts[part][at:at + 1]

    away = (1 - z_hi) * BL + bl
    for channel in range(2):
        first_out[channel] = start_gains[pl.ds(pl.multiple_of(channel * 128 + away * 8, 8), 8), :]

    neighbours = jnp.where(above, LINE, 0) + jnp.where(below, LINE, 0)
    pl.semaphore_wait(barrier, RING - 1 + LINE - 1 + neighbours)

    sends = []

    def remote(src, dst, send, recv, device):
        return pltpu.make_async_remote_copy(
            src_ref=src, dst_ref=dst, send_sem=send, recv_sem=recv, device_id=device, device_id_type=MESH)

    param_copies = []
    for step in (4, 3, 5, 2, 6, 1, 7):
        device = {"bl": lax.rem(bl + step, BL)}
        for outgoing, send, recv in ((params, s_param, r_param), (ids, s_ids, r_ids)):
            copy = remote(outgoing.at[bl], outgoing.at[bl], send.at[step], recv.at[step], device)
            copy.start()
            param_copies.append(copy)
    sends.extend(param_copies)
    first_copy = remote(first_out, first_in, s_first, r_first, ring(BL)[1])
    first_copy.start()
    sends.append(first_copy)
    for copy in param_copies:
        copy.wait_recv()
    for device in range(BL):
        counts[device:device + 1, :] = ids[device, 2:3, :]
    scalars = [pltpu.make_async_copy(counts, counts_scalar, s_load.at[4]),
               pltpu.make_async_copy(params, params_scalar, s_load.at[5])]
    for copy in scalars:
        copy.start()
    for copy in scalars:
        copy.wait()

    ratio_zero, ratio_one = ratio_of(freq * 2), ratio_of(freq * 2 + 1)
    relative = ratio_one / ratio_zero
    u, v, w = coords[0] * ratio_zero, coords[1] * ratio_zero, coords[2] * ratio_zero

    def lives_of(patch):
        return counts_scalar[patch >> 1, patch & 1]

    def one_component(component, state):
        sums, (patch, slot, live) = list(state[0:4]), state[4:7]
        device, column = patch >> 1, (patch & 1) * 64 + slot
        delay = (u * params_scalar[device, 0, column] + v * params_scalar[device, 1, column]
                 + w * params_scalar[device, 2, column])
        keep = jnp.where(slot == 0, 0.0, 1.0)
        for channel, turns in enumerate((delay, delay * relative)):
            turns = turns - jnp.round(turns)
            square = turns * turns
            sine = turns * factored(SIN_FACTORS, square)
            scaled = sine * params_scalar[device, 3 + channel, column]
            sums[2 * channel] = sums[2 * channel] * keep + scaled * sine
            sums[2 * channel + 1] = sums[2 * channel + 1] * keep + scaled * factored(COS_FACTORS, square)
        for place in range(4):
            running[component, place] = sums[place]
        done = slot + 1 >= live
        patch = jnp.minimum(patch + jnp.where(done, 1, 0), DIRS - 1)
        slot = jnp.where(done, 0, slot + 1)
        return (*sums, patch, slot, lives_of(patch))

    zero = jnp.zeros((TIMES, LANES), F32)
    start = jnp.int32(0)
    lax.fori_loop(0, COMPONENTS, one_component, (zero,) * 4 + (start, start, lives_of(start)), unroll=32)

    def finish_patch(patch, end):
        end = end + lives_of(patch)
        last = jnp.clip(end - 1, 0, COMPONENTS - 1)
        for channel in range(2):
            total = params_scalar[patch >> 1, 5, (patch & 1) * 2 + channel]
            model[channel, patch, 0] = total - (2.0 * SIN_SCALE * SIN_SCALE) * running[last, 2 * channel]
            model[channel, patch, 1] = (-2.0 * SIN_SCALE * COS_SCALE) * running[last, 2 * channel + 1]
        return end

    lax.fori_loop(0, DIRS, finish_patch, start, unroll=True)

    def chip_of(offset):
        return lax.rem(z_lo + offset, LINE)

    def corrupted(row, wait=None):
        totals = [jnp.zeros((TIMES, LANES), F32) for _ in range(4)]
        for offset in (2, 1, 3, 0):
            if wait is not None:
                wait(offset)
            for slot, (z, which) in enumerate(places):
                patch = z * BL + chip_of(offset) * 2 + which
                for channel in range(2):
                    jr, ji = row(offset, slot, channel), row(offset, slot, 2 + channel)
                    mr, mi = model[channel, patch, 0], model[channel, patch, 1]
                    totals[2 * channel] += jr * mr - ji * mi
                    totals[2 * channel + 1] += jr * mi + ji * mr
        return totals

    def row_at_start(ref):
        return lambda offset, slot, at: ref[offset, slot, at:at + 1, :]

    def row_at(round_index):
        if round_index == 0:
            return row_at_start(joint_start)
        return lambda offset, slot, at: joint_in[offset][round_index - 1, slot, at:at + 1, :]

    totals = corrupted(row_at_start(joint_true))
    for channel in range(2):
        for part in range(2):
            observed[channel, part] = noise[pl.ds(channel * 32 + part, TIMES, stride=2), :] + totals[2 * channel + part]

    def put_energy(patch, _):
        for channel in range(2):
            mr, mi = model[channel, patch, 0], model[channel, patch, 1]
            row = jnp.sum(mr * mr + mi * mi, axis=0, keepdims=True)
            weight = jnp.full((1, LANES), 1.0, F32) * (1.0 - flags[channel].astype(F32))
            for part in range(2):
                at = part * 2 + channel
                energy[patch, at:at + 1, :] = row
                energy[patch, 4 + at:5 + at, :] = weight
        return 0

    lax.fori_loop(0, DIRS, put_energy, 0, unroll=True)

    def ring_copy(src, dst, send, recv, other):
        return remote(src, dst, send.at[other], recv.at[me], ring_device(other))

    def send_ring(src, dst, send, recv, other):
        copy = ring_copy(src, dst, send, recv, other)
        copy.start()
        sends.append(copy)

    def wait_ring(landing, send, recv, other):
        remote(landing, landing, send.at[other], recv.at[other], ring_device(other)).wait_recv()

    def others_of(offset):
        some = ((1 - z_hi, 0), (1 - z_hi, 1), (z_hi, 1 - core)) if offset == 0 else places
        return [(z * 2 + which, z * BL + chip_of(offset) * 2 + which) for z, which in some]

    own_slot = z_hi * 2 + core

    def send_offset(outgoing, incoming, send, recv, turn, offset):
        back = (LINE - offset) % LINE
        for slot, other in others_of(offset):
            copy = remote(outgoing[offset].at[turn, slot], incoming[back].at[turn, own_slot],
                          send.at[turn, offset * 4 + slot], recv.at[turn, back * 4 + own_slot], ring_device(other))
            copy.start()
            sends.append(copy)
        if offset == 0:
            incoming[0][turn, own_slot] = outgoing[0][turn, own_slot]

    def wait_offset(incoming, send, recv, turn, offset):
        for slot, other in others_of(offset):
            landed = incoming[offset].at[turn, slot]
            remote(landed, landed, send.at[turn, offset * 4 + slot], recv.at[turn, offset * 4 + slot],
                   ring_device(other)).wait_recv()


    row8 = lax.broadcasted_iota(jnp.int32, (8, LANES), 0)
    is_real = (row8 & 2) == 0

    def from_later(value):
        return pltpu.roll(value, 6, 0)

    def from_earlier(value):
        return pltpu.roll(value, 2, 0)

    def swapped(value):
        return jnp.where(is_real, from_later(value), from_earlier(value))

    def split_rows(gains):
        return jnp.concatenate(split_two(jnp.concatenate([
            jnp.concatenate([gains[0:4], gains[8:12]], axis=0),
            jnp.concatenate([gains[4:8], gains[12:16]], axis=0)], axis=1)), axis=0)

    def put_ends(rows, chip):
        columns = onehot[:, pl.ds(pl.multiple_of(chip * 512, 512), 512)]
        both = jnp.dot(rows, columns, preferred_element_type=F32)
        both = both[0:8] + both[8:16]
        pairs = []
        for which in range(2):
            start = which * 2 * LANES
            near, far = both[:, start:start + LANES], both[:, start + LANES:start + 2 * LANES]
            firsts[chip * 2 + which] = near
            seconds[chip * 2 + which] = far
            pairs.append((near, far))
        return pairs

    def to_halves(rows):
        return jnp.concatenate([
            rows[0:4, 0:256], rows[0:4, 256:512], rows[4:8, 0:256], rows[4:8, 256:512]], axis=0)

    here = lax.broadcasted_iota(jnp.int32, (16, 128), 0)
    there = lax.broadcasted_iota(jnp.int32, (16, 128), 1)
    slot = there >> 3
    slot_y = jnp.where(slot < 8, 0, jnp.where(slot < 12, 1, -1))
    slot_z = jnp.where(slot < 8, slot & 1, jnp.where(slot < 12, 1, 0))
    slot_x = jnp.where(slot < 8, slot >> 1, slot & 3)
    apart = (16 * slot_y + 8 * ((here >> 3) - slot_z) + 2 * (x - slot_x) + (here & 1) - (there & 1)).astype(F32)
    reached = jnp.where((here & 6) == (there & 6), jnp.where(jnp.abs(apart) <= REACH, 1.0, 0.0), 0.0)
    smoothing = jnp.exp(-(apart * apart) / (2.0 * SPREAD * SPREAD)) * reached

    smoothing_high, smoothing_low = split_two(smoothing)
    smoothing_both = jnp.concatenate([smoothing_high, smoothing_low], axis=0)

    def wait_joint(round_index):
        if round_index == 0:
            return None
        return lambda offset: wait_offset(joint_in, s_joint, r_joint, round_index - 1, offset)

    def fit_and_send(turn):
        row = row_at(turn)
        totals = corrupted(row, wait_joint(turn))
        rests = [observed[place // 2, place % 2] - totals[place] for place in range(4)]
        for offset in (0, 1, 3, 2):
            for slot, (z, which) in enumerate(places):
                patch = z * BL + chip_of(offset) * 2 + which
                for channel in range(2):
                    rest_r, rest_i = rests[2 * channel], rests[2 * channel + 1]
                    mr, mi = model[channel, patch, 0], model[channel, patch, 1]
                    power = energy[patch, channel:channel + 1, :]
                    for part, value in enumerate((mr * rest_r + mi * rest_i, mr * rest_i - mi * rest_r)):
                        at = part * 2 + channel
                        fits[offset][turn, slot, at:at + 1, :] = (
                            jnp.sum(value, axis=0, keepdims=True) + row(offset, slot, at) * power)
            send_offset(fits, fits_in, s_fit, r_fit, turn, offset)

    inverse = None
    weight_halves = None
    weight_rows = None
    for turn in range(ITERS):
        fit_and_send(turn)
        if turn == 0:
            for step in FAR + NEAR[:-1]:
                other = ring(step)[0]
                send_ring(energy.at[other], energy_in.at[me], s_energy, r_energy, other)
            energy_in[me] = energy[me]
            for source in range(BL):
                for end in range(2):
                    row = ids[source, end:end + 1, :]
                    start = (source * 2 + end) * LANES
                    onehot[:, start:start + LANES] = jnp.where(station == row, 1.0, 0.0).astype(BF16)
            first_copy.wait_recv()
            for channel in range(2):
                own = start_gains[pl.ds(pl.multiple_of(channel * 128 + me * 8, 8), 8), :]
                other = first_in[channel]
                for row in range(8):
                    half, lane, part = row // 4, (row // 2) % 2, row % 2
                    at = half * 4 + part * 2 + channel
                    owned[z_hi, at:at + 1, lane * LANES:(lane + 1) * LANES] = own[row:row + 1]
                    owned[1 - z_hi, at:at + 1, lane * LANES:(lane + 1) * LANES] = other[row:row + 1]
            gains_now = owned[...].reshape(16, 256)
            rows = split_rows(gains_now)
            for chip in range(LINE):
                put_ends(rows, chip)
            for step in NEAR[:-1] + FAR:
                other = ring(step)[0]
                wait_ring(energy_in.at[other], s_energy, r_energy, other)
            weight_rows = jnp.concatenate([energy_in[0, 4:8], energy_in[BL, 4:8]], axis=0)
            weight_rows = jnp.concatenate([weight_rows] * 4, axis=1)
            weight_halves = to_halves(weight_rows)

        received = jnp.zeros((32, STATIONS), F32)
        for offset in (2, 1, 3, 0):
            chip = chip_of(offset)
            wait_offset(fits_in, s_fit, r_fit, turn, offset)
            columns = []
            for which in range(2):
                source = chip * 2 + which
                fit = jnp.concatenate([fits_in[offset][turn, which], fits_in[offset][turn, 2 + which]], axis=0)
                power = jnp.concatenate([energy_in[source, 0:4], energy_in[BL + source, 0:4]], axis=0)
                for toward_first in (True, False):
                    far = (seconds if toward_first else firsts)[source]
                    far_swapped = swapped(far)
                    direct = far * fit
                    crossed = far_swapped * fit
                    if toward_first:
                        numer = jnp.where(is_real, direct - from_later(direct), crossed + from_earlier(crossed))
                    else:
                        numer = jnp.where(is_real, direct + from_later(direct), from_earlier(crossed) - crossed)
                    denom = (far * far + far_swapped * far_swapped) * power
                    columns.append(jnp.concatenate(split_two(jnp.concatenate([numer, denom], axis=0)), axis=0))
            received = received + lax.dot_general(
                jnp.concatenate(columns, axis=1), onehot[:, pl.ds(pl.multiple_of(chip * 512, 512), 512)],
                (((1,), (1,)), ((), ())), preferred_element_type=F32)
        received = received[0:16] + received[16:32]
        solved = (received[0:8] * weight_rows) / jnp.maximum(received[8:16] * weight_rows, 1.0)
        blended = 0.5 * gains_now + 0.5 * to_halves(solved)
        packed = weight_halves * blended

        width = 384 if turn == 0 else 256
        for z in range(2):
            mixed[turn, 2 * x + z, :, 0:256] = packed[z * 8:z * 8 + 8]
            if turn == 0:
                mixed[turn, 2 * x + z, :, 256:384] = weight_halves[z * 8:z * 8 + 8, 0:LANES]

        def planes(first, count):
            return mixed.at[turn, pl.ds(first, count), :, pl.ds(0, width)]

        def far_plane(index):
            return mixed_far.at[turn, pl.ds(index, 1), :, pl.ds(0, width)]

        line_copies, far_copies = [], []
        for other_x in range(LINE):
            up = remote(planes(2 * x + 1, 1), far_plane(x), s_mix.at[turn, 3 + other_x],
                        r_mix.at[turn, 4 + x], plane(y + 1, other_x))
            down = remote(planes(2 * x, 1), far_plane(4 + x), s_mix.at[turn, 7 + other_x],
                          r_mix.at[turn, 8 + x], plane(y - 1, other_x))
            far_copies.append((jnp.logical_and(above, other_x <= x), up))
            far_copies.append((jnp.logical_and(below, other_x >= x), down))
        for needed, copy in far_copies:
            pl.when(needed)(copy.start)
        for step in (2, 1, 3):
            copy = remote(planes(2 * x, 2), planes(2 * x, 2), s_mix.at[turn, step - 1], r_mix.at[turn, x],
                          plane(y, lax.rem(x + step, LINE)))
            copy.start()
            line_copies.append(copy)

        for step in range(1, LINE):
            source_x = lax.rem(x + step, LINE)
            remote(planes(2 * source_x, 2), planes(2 * source_x, 2), s_mix.at[turn, step - 1],
                   r_mix.at[turn, source_x], plane(y, source_x)).wait_recv()

        def smoothed(planes_now, first):
            high, low = split_two(planes_now[turn, :, :, 0:width].reshape(64, width))
            both = jnp.dot(smoothing_both[:, first:first + 64], high, preferred_element_type=F32)
            return both[0:16] + both[16:32] + jnp.dot(smoothing_high[:, first:first + 64], low, preferred_element_type=F32)

        summed = smoothed(mixed, 0)
        for source_x in range(LINE):
            from_above = remote(far_plane(4 + source_x), far_plane(4 + source_x), s_mix.at[turn, 3 + source_x],
                                r_mix.at[turn, 8 + source_x], plane(y + 1, source_x))
            from_below = remote(far_plane(source_x), far_plane(source_x), s_mix.at[turn, 7 + source_x],
                                r_mix.at[turn, 4 + source_x], plane(y - 1, source_x))
            pl.when(jnp.logical_and(above, source_x <= x))(from_above.wait_recv)
            pl.when(jnp.logical_and(below, source_x >= x))(from_below.wait_recv)
        summed = summed + smoothed(mixed_far, 64)
        if turn == 0:
            inverse = 1.0 / jnp.maximum(summed[:, 256:384], 1.0)
            inverse = jnp.concatenate([inverse, inverse], axis=1)
        gains_now = summed[:, 0:256] * inverse

        earlier = len(sends)
        if turn == ITERS - 1:
            for z in range(2):
                for channel in range(2):
                    for row in range(8):
                        half, lane, part = row // 4, (row // 2) % 2, row % 2
                        at = z * 8 + half * 4 + part * 2 + channel
                        stage[z, channel, row:row + 1, :] = gains_now[at:at + 1, lane * LANES:(lane + 1) * LANES]
            for step in FAR + NEAR[:-1]:
                other = ring(step)[0]
                send_ring(stage.at[lax.div(other, BL)], gains_out.at[:, me], s_gain, r_gain, other)
            gains_out[:, me] = stage[z_hi]

        rows = split_rows(gains_now)
        for offset in (0, 1, 3, 2):
            chip = chip_of(offset)
            for which, (near, far) in enumerate(put_ends(rows, chip)):
                direct = near * far
                crossed = near * swapped(far)
                joint = jnp.where(is_real, direct + from_later(direct), crossed - from_earlier(crossed))
                joint_out[offset][turn, which] = joint[0:4]
                joint_out[offset][turn, 2 + which] = joint[4:8]
            send_offset(joint_out, joint_in, s_joint, r_joint, turn, offset)
        if turn == ITERS - 1:
            for copy in sends[:earlier]:
                copy.wait_send()

        for copy in line_copies:
            copy.wait_send()
        for needed, copy in far_copies:
            pl.when(needed)(copy.wait_send)

    totals = corrupted(row_at(ITERS), wait_joint(ITERS))
    for channel in range(2):
        for part in range(2):
            residual_out[pl.ds(channel * 32 + part, TIMES, stride=2), :] = (
                observed[channel, part] - totals[2 * channel + part])
    for step in NEAR[:-1] + FAR:
        other = ring(step)[0]
        wait_ring(gains_out.at[:, other], s_gain, r_gain, other)
    for copy in sends[earlier:]:
        copy.wait_send()


def local(visibility_noise, baseline_wavelength_coords, station_pair, comp_position, comp_flux,
          comp_spectral, comp_count, true_gains, start_gains, channel_flags):
    vmem = pl.BlockSpec(memory_space=VMEM)
    smem = pl.BlockSpec(memory_space=SMEM)
    anywhere = pl.BlockSpec(memory_space=pltpu.MemorySpace.HBM)
    dma = pltpu.SemaphoreType.DMA
    def tiles(gains):
        return gains.reshape(2, DIRS, 2, 4, LANES).transpose(0, 1, 3, 2, 4).reshape(2 * DIRS * 8, LANES)

    gains, residual = pl.pallas_call(
        calibrate_kernel,
        out_shape=(pltpu.VMEM((2, DIRS, 8, LANES), F32), pltpu.VMEM((64, LANES), F32)),
        in_specs=[anywhere, anywhere, vmem, vmem, vmem, vmem, smem, anywhere, anywhere, smem],
        out_specs=(vmem, vmem),
        scratch_shapes=[
            pltpu.VMEM((64, LANES), F32),
            pltpu.VMEM((3, TIMES, LANES), F32),
            pltpu.VMEM((256, LANES), F32),
            pltpu.VMEM((256, LANES), F32),
            pltpu.VMEM((BL, 8, LANES), F32),
            pltpu.VMEM((BL, 8, LANES), jnp.int32),
            pltpu.VMEM((BL, LANES), jnp.int32),
            pltpu.SMEM((BL, 8, LANES), F32),
            pltpu.SMEM((BL, LANES), jnp.int32),
            pltpu.VMEM((COMPONENTS, 4, TIMES, LANES), F32),
            pltpu.VMEM((2, DIRS, 2, TIMES, LANES), F32),
            pltpu.VMEM((STATIONS, 2 * LANES), BF16),
            pltpu.VMEM((STATIONS, BL * 2 * LANES), BF16),
            pltpu.VMEM((2, 2, TIMES, LANES), F32),
            pltpu.VMEM((LINE, 4, 4, LANES), F32),
            pltpu.VMEM((BL, 8, LANES), F32),
            pltpu.VMEM((BL, 8, LANES), F32),
            pltpu.VMEM((2, 8, 256), F32),
            pltpu.VMEM((2, 8, LANES), F32),
            pltpu.VMEM((2, 8, LANES), F32),
            pltpu.VMEM((RING, 8, LANES), F32),
            pltpu.VMEM((RING, 8, LANES), F32),
            pltpu.VMEM((LINE, 4, 4, LANES), F32),
        ] + [pltpu.VMEM((ITERS, 4, 4, LANES), F32)] * 16 + [
            pltpu.VMEM((ITERS, 8, 8, 384), F32),
            pltpu.VMEM((ITERS, 8, 8, 384), F32),
            pltpu.VMEM((2, 2, 8, LANES), F32),
            dma((6,)), dma((BL,)), dma((BL,)), dma((BL,)), dma((BL,)),
            dma(()), dma(()),
            dma((RING,)), dma((RING,)),
            dma((ITERS, RING)), dma((ITERS, RING)),
            dma((ITERS, RING)), dma((ITERS, RING)),
            dma((ITERS, 11)), dma((ITERS, 12)),
            dma((RING,)), dma((RING,)),
        ],
        compiler_params=pltpu.CompilerParams(
            collective_id=0, has_side_effects=True, vmem_limit_bytes=56 * 1024 * 1024),
        name="calibrate",
    )(visibility_noise.reshape(64, LANES), baseline_wavelength_coords, station_pair, comp_position, comp_flux,
      comp_spectral, comp_count, tiles(true_gains), tiles(start_gains), channel_flags)
    gains = gains.reshape(2, DIRS, 4, 2, LANES).transpose(0, 1, 3, 2, 4).reshape(2, DIRS, 2, STATIONS)
    return gains, residual.reshape(2, TIMES, 2, LANES)


def solution(mesh):
    in_specs = (
        P("freq", None, None, "bl"),
        P(None, None, "bl"),
        P(None, "bl"),
        P("bl", None, None),
        P("bl", None),
        P("bl", None),
        P("bl"),
        P("freq", None, None, None),
        P("freq", None, None, None),
        P("freq"),
    )
    out_specs = (P("freq", None, None, None), P("freq", None, None, "bl"))
    return jax.shard_map(local, mesh=mesh, in_specs=in_specs, out_specs=out_specs, check_vma=False)
```

```python
import jax
import jax.numpy as jnp
from jax import lax
from jax.experimental import pallas as pl
from jax.experimental.pallas import tpu as pltpu
from jax.sharding import PartitionSpec as P

F32 = jnp.float32
BF16 = jnp.bfloat16
MESH = pl.DeviceIdType.MESH
VMEM = pltpu.MemorySpace.VMEM
SMEM = pltpu.MemorySpace.SMEM

NEAR = (1, 15, 2, 14, 3, 13, 4, 12, 0)
FAR = (8, 7, 9, 6, 10, 5, 11)
BL = 8
LINE = 4
RING = 16
ITERS = 3
DIRS = 16
TIMES = 16
STATIONS = 512
COMPONENTS = 512
LANES = 128
REACH = 8.0
SPREAD = 4.0

SIN_SCALE, SIN_FACTORS = -0.5546349618, (-0.978320908350836, -3.6046909402902565, 5.789750187942454)
COS_SCALE, COS_FACTORS = -1.2221263189, (-0.24999786765951873, -3.0567664626737323, 3.2729900649797434)


def factored(factors, at):
    return (at + factors[0]) * (at * (at + factors[1]) + factors[2])


def split_two(value):
    high = value.astype(BF16)
    low = (value - high.astype(F32)).astype(BF16)
    return high, low


def ratio_of(channel):
    return 0.5 + (channel.astype(F32) + 0.5) / 128.0


def calibrate_kernel(noise_hbm, coords_hbm, pair, position, flux, spectral, count, true_hbm, start_hbm, flags,
                     gains_out, residual_out,
                     noise, coords, true_gains, start_gains, params, ids, counts, params_scalar, counts_scalar, running, model,
                     own_onehot, onehot, observed, joint_true, firsts, seconds, owned, first_out, first_in,
                     energy, energy_in, joint_start, joint_apart,
                     fits_0, fits_1, fits_2, fits_3, fits_in_0, fits_in_1, fits_in_2, fits_in_3,
                     joint_out_0, joint_out_1, joint_out_2, joint_out_3, joint_in_0, joint_in_1, joint_in_2, joint_in_3,
                     mixed, mixed_far, stage,
                     s_load, s_param, r_param, s_ids, r_ids,
                     s_first, r_first, s_energy, r_energy, s_fit, r_fit, s_joint, r_joint,
                     s_mix, r_mix, s_gain, r_gain):
    freq = lax.axis_index("freq")
    bl = lax.axis_index("bl")
    y = lax.div(freq, 8)
    z_hi = lax.rem(lax.div(freq, LINE), 2)
    x = lax.rem(freq, LINE)
    me = z_hi * BL + bl
    above, below = y < lax.axis_size("freq") // 8 - 1, y > 0

    z_lo, core = lax.div(bl, 2), lax.rem(bl, 2)
    fits = (fits_0, fits_1, fits_2, fits_3)
    fits_in = (fits_in_0, fits_in_1, fits_in_2, fits_in_3)
    joint_out = (joint_out_0, joint_out_1, joint_out_2, joint_out_3)
    joint_in = (joint_in_0, joint_in_1, joint_in_2, joint_in_3)
    places = ((0, 0), (0, 1), (1, 0), (1, 1))

    def ring_device(other):
        return {"freq": (y * 2 + lax.div(other, BL)) * LINE + x, "bl": lax.rem(other, BL)}

    def ring(step):
        other = lax.rem(me + step, RING)
        return other, ring_device(other)

    def plane(other_y, other_x):
        return {"freq": (other_y * 2 + z_hi) * LINE + other_x, "bl": bl}

    loads = []
    for index, (source, target) in enumerate((
            (true_hbm, true_gains), (start_hbm, start_gains), (noise_hbm, noise), (coords_hbm, coords))):
        copy = pltpu.make_async_copy(source, target, s_load.at[index])
        copy.start()
        loads.append(copy)

    mixed_far[...] = jnp.zeros(mixed_far.shape, F32)

    barrier = pltpu.get_barrier_semaphore()
    for step in range(1, RING):
        pl.semaphore_signal(barrier, inc=1, device_id=ring(step)[1], device_id_type=MESH)
    for step in range(1, LINE):
        pl.semaphore_signal(barrier, inc=1, device_id=plane(y, lax.rem(x + step, LINE)), device_id_type=MESH)

    @pl.when(above)
    def _():
        for other_x in range(LINE):
            pl.semaphore_signal(barrier, inc=1, device_id=plane(y + 1, other_x), device_id_type=MESH)

    @pl.when(below)
    def _():
        for other_x in range(LINE):
            pl.semaphore_signal(barrier, inc=1, device_id=plane(y - 1, other_x), device_id_type=MESH)

    def both(values):
        return jnp.concatenate([values[0:1], values[1:2]], axis=1)

    l, m = both(position[:, 0, :]), both(position[:, 1, :])
    square = l * l + m * m
    params[bl, 0:1, :] = l
    params[bl, 1:2, :] = m
    params[bl, 2:3, :] = -square / (1.0 + jnp.sqrt(1.0 - square))
    lane = lax.broadcasted_iota(jnp.int32, (1, LANES), 1)
    lives = jnp.where(lane < 64, count[0], count[1])
    fluxes = jnp.where((lane & 63) < lives, both(flux[...]), 0.0)
    index = both(spectral[...])
    extra = jnp.zeros((1, LANES), F32)
    for channel in range(2):
        ratio = jnp.full((1, LANES), 1.0, F32) * ratio_of(freq * 2 + channel)
        spectrum = fluxes * jnp.exp(index * jnp.log(ratio))
        params[bl, 3 + channel:4 + channel, :] = spectrum
        for half in range(2):
            total = jnp.sum(jnp.where((lane >> 6) == half, spectrum, 0.0), axis=1, keepdims=True)
            extra = jnp.where(lane == half * 2 + channel, total, extra)
    params[bl, 5:6, :] = extra
    ids[bl, 0:2, :] = pair[...]
    ids[bl, 2:3, :] = jnp.where(lane == 0, count[0], count[1])

    station = lax.broadcasted_iota(jnp.int32, (STATIONS, LANES), 0)
    for end in range(2):
        own_onehot[:, end * LANES:(end + 1) * LANES] = jnp.where(station == pair[end:end + 1, :], 1.0, 0.0).astype(BF16)
    for copy in loads:
        copy.wait()

    def local_joint(gains):
        rows = []
        for part in range(2):
            rows.append(jnp.concatenate(
                [gains[pl.ds(tile * 2 + part, 32, stride=8), :] for tile in range(4)], axis=1))
        high, low = split_two(jnp.concatenate(rows, axis=0))
        ends = jnp.dot(jnp.concatenate([high, low], axis=0), own_onehot[...], preferred_element_type=F32)
        ends = ends[0:64] + ends[64:128]
        pr, pi = ends[0:32, 0:LANES], ends[32:64, 0:LANES]
        qr, qi = ends[0:32, LANES:], ends[32:64, LANES:]
        return pr * qr + pi * qi, pi * qr - pr * qi

    true_parts, start_parts = local_joint(true_gains), local_joint(start_gains)
    apart_parts = [true_parts[part] - start_parts[part] for part in range(2)]
    for ref, parts in ((joint_true, true_parts), (joint_start, start_parts), (joint_apart, apart_parts)):
        for channel in range(2):
            for part in range(2):
                for patch in range(DIRS):
                    at = channel * DIRS + patch
                    offset = lax.rem((patch % BL) // 2 + LINE - z_lo, LINE)
                    slot = (patch // BL) * 2 + patch % 2
                    ref[offset, slot, part * 2 + channel:part * 2 + channel + 1, :] = parts[part][at:at + 1]

    away = (1 - z_hi) * BL + bl
    for channel in range(2):
        first_out[channel] = start_gains[pl.ds(pl.multiple_of(channel * 128 + away * 8, 8), 8), :]

    neighbours = jnp.where(above, LINE, 0) + jnp.where(below, LINE, 0)
    pl.semaphore_wait(barrier, RING - 1 + LINE - 1 + neighbours)

    sends = []

    def remote(src, dst, send, recv, device):
        return pltpu.make_async_remote_copy(
            src_ref=src, dst_ref=dst, send_sem=send, recv_sem=recv, device_id=device, device_id_type=MESH)

    param_copies = []
    for step in (4, 3, 5, 2, 6, 1, 7):
        device = {"bl": lax.rem(bl + step, BL)}
        for outgoing, send, recv in ((params, s_param, r_param), (ids, s_ids, r_ids)):
            copy = remote(outgoing.at[bl], outgoing.at[bl], send.at[step], recv.at[step], device)
            copy.start()
            param_copies.append(copy)
    sends.extend(param_copies)
    first_copy = remote(first_out, first_in, s_first, r_first, ring(BL)[1])
    first_copy.start()
    sends.append(first_copy)
    for copy in param_copies:
        copy.wait_recv()
    for device in range(BL):
        counts[device:device + 1, :] = ids[device, 2:3, :]
    scalars = [pltpu.make_async_copy(counts, counts_scalar, s_load.at[4]),
               pltpu.make_async_copy(params, params_scalar, s_load.at[5])]
    for copy in scalars:
        copy.start()
    for copy in scalars:
        copy.wait()

    ratio_zero, ratio_one = ratio_of(freq * 2), ratio_of(freq * 2 + 1)
    relative = ratio_one / ratio_zero
    u, v, w = coords[0] * ratio_zero, coords[1] * ratio_zero, coords[2] * ratio_zero

    def lives_of(patch):
        return counts_scalar[patch >> 1, patch & 1]

    def one_component(component, state):
        sums, (patch, slot, live) = list(state[0:4]), state[4:7]
        device, column = patch >> 1, (patch & 1) * 64 + slot
        delay = (u * params_scalar[device, 0, column] + v * params_scalar[device, 1, column]
                 + w * params_scalar[device, 2, column])
        keep = jnp.where(slot == 0, 0.0, 1.0)
        for channel, turns in enumerate((delay, delay * relative)):
            turns = turns - jnp.round(turns)
            square = turns * turns
            sine = turns * factored(SIN_FACTORS, square)
            scaled = sine * params_scalar[device, 3 + channel, column]
            sums[2 * channel] = sums[2 * channel] * keep + scaled * sine
            sums[2 * channel + 1] = sums[2 * channel + 1] * keep + scaled * factored(COS_FACTORS, square)
        for place in range(4):
            running[component, place] = sums[place]
        done = slot + 1 >= live
        patch = jnp.minimum(patch + jnp.where(done, 1, 0), DIRS - 1)
        slot = jnp.where(done, 0, slot + 1)
        return (*sums, patch, slot, lives_of(patch))

    zero = jnp.zeros((TIMES, LANES), F32)
    start = jnp.int32(0)
    lax.fori_loop(0, COMPONENTS, one_component, (zero,) * 4 + (start, start, lives_of(start)), unroll=32)

    def finish_patch(patch, end):
        end = end + lives_of(patch)
        last = jnp.clip(end - 1, 0, COMPONENTS - 1)
        for channel in range(2):
            total = params_scalar[patch >> 1, 5, (patch & 1) * 2 + channel]
            model[channel, patch, 0] = total - (2.0 * SIN_SCALE * SIN_SCALE) * running[last, 2 * channel]
            model[channel, patch, 1] = (-2.0 * SIN_SCALE * COS_SCALE) * running[last, 2 * channel + 1]
        return end

    lax.fori_loop(0, DIRS, finish_patch, start, unroll=True)

    def chip_of(offset):
        return lax.rem(z_lo + offset, LINE)

    def corrupted(row, wait=None):
        totals = [jnp.zeros((TIMES, LANES), F32) for _ in range(4)]
        for offset in (2, 1, 3, 0):
            if wait is not None:
                wait(offset)
            for slot, (z, which) in enumerate(places):
                patch = z * BL + chip_of(offset) * 2 + which
                for channel in range(2):
                    jr, ji = row(offset, slot, channel), row(offset, slot, 2 + channel)
                    mr, mi = model[channel, patch, 0], model[channel, patch, 1]
                    totals[2 * channel] += jr * mr - ji * mi
                    totals[2 * channel + 1] += jr * mi + ji * mr
        return totals

    def row_at_start(ref):
        return lambda offset, slot, at: ref[offset, slot, at:at + 1, :]

    def row_at(round_index):
        if round_index == 0:
            return row_at_start(joint_start)
        return lambda offset, slot, at: joint_in[offset][round_index - 1, slot, at:at + 1, :]

    def put_energy(patch, _):
        for channel in range(2):
            mr, mi = model[channel, patch, 0], model[channel, patch, 1]
            row = jnp.sum(mr * mr + mi * mi, axis=0, keepdims=True)
            weight = jnp.full((1, LANES), 1.0, F32) * (1.0 - flags[channel].astype(F32))
            for part in range(2):
                at = part * 2 + channel
                energy[patch, at:at + 1, :] = row
                energy[patch, 4 + at:5 + at, :] = weight
        return 0

    lax.fori_loop(0, DIRS, put_energy, 0, unroll=True)

    def ring_copy(src, dst, send, recv, other):
        return remote(src, dst, send.at[other], recv.at[me], ring_device(other))

    def send_ring(src, dst, send, recv, other):
        copy = ring_copy(src, dst, send, recv, other)
        copy.start()
        sends.append(copy)

    def wait_ring(landing, send, recv, other):
        remote(landing, landing, send.at[other], recv.at[other], ring_device(other)).wait_recv()

    def others_of(offset):
        some = ((1 - z_hi, 0), (1 - z_hi, 1), (z_hi, 1 - core)) if offset == 0 else places
        return [(z * 2 + which, z * BL + chip_of(offset) * 2 + which) for z, which in some]

    own_slot = z_hi * 2 + core

    def send_offset(outgoing, incoming, send, recv, turn, offset):
        back = (LINE - offset) % LINE
        for slot, other in others_of(offset):
            copy = remote(outgoing[offset].at[turn, slot], incoming[back].at[turn, own_slot],
                          send.at[turn, offset * 4 + slot], recv.at[turn, back * 4 + own_slot], ring_device(other))
            copy.start()
            sends.append(copy)
        if offset == 0:
            incoming[0][turn, own_slot] = outgoing[0][turn, own_slot]

    def wait_offset(incoming, send, recv, turn, offset):
        for slot, other in others_of(offset):
            landed = incoming[offset].at[turn, slot]
            remote(landed, landed, send.at[turn, offset * 4 + slot], recv.at[turn, offset * 4 + slot],
                   ring_device(other)).wait_recv()


    row8 = lax.broadcasted_iota(jnp.int32, (8, LANES), 0)
    is_real = (row8 & 2) == 0

    def from_later(value):
        return pltpu.roll(value, 6, 0)

    def from_earlier(value):
        return pltpu.roll(value, 2, 0)

    def swapped(value):
        return jnp.where(is_real, from_later(value), from_earlier(value))

    def split_rows(gains):
        return jnp.concatenate(split_two(jnp.concatenate([
            jnp.concatenate([gains[0:4], gains[8:12]], axis=0),
            jnp.concatenate([gains[4:8], gains[12:16]], axis=0)], axis=1)), axis=0)

    def put_ends(rows, chip):
        columns = onehot[:, pl.ds(pl.multiple_of(chip * 512, 512), 512)]
        both = jnp.dot(rows, columns, preferred_element_type=F32)
        both = both[0:8] + both[8:16]
        pairs = []
        for which in range(2):
            start = which * 2 * LANES
            near, far = both[:, start:start + LANES], both[:, start + LANES:start + 2 * LANES]
            firsts[chip * 2 + which] = near
            seconds[chip * 2 + which] = far
            pairs.append((near, far))
        return pairs

    def to_halves(rows):
        return jnp.concatenate([
            rows[0:4, 0:256], rows[0:4, 256:512], rows[4:8, 0:256], rows[4:8, 256:512]], axis=0)

    here = lax.broadcasted_iota(jnp.int32, (16, 128), 0)
    there = lax.broadcasted_iota(jnp.int32, (16, 128), 1)
    slot = there >> 3
    slot_y = jnp.where(slot < 8, 0, jnp.where(slot < 12, 1, -1))
    slot_z = jnp.where(slot < 8, slot & 1, jnp.where(slot < 12, 1, 0))
    slot_x = jnp.where(slot < 8, slot >> 1, slot & 3)
    apart = (16 * slot_y + 8 * ((here >> 3) - slot_z) + 2 * (x - slot_x) + (here & 1) - (there & 1)).astype(F32)
    reached = jnp.where((here & 6) == (there & 6), jnp.where(jnp.abs(apart) <= REACH, 1.0, 0.0), 0.0)
    smoothing = jnp.exp(-(apart * apart) / (2.0 * SPREAD * SPREAD)) * reached

    smoothing_high, smoothing_low = split_two(smoothing)
    smoothing_both = jnp.concatenate([smoothing_high, smoothing_low], axis=0)

    def wait_joint(round_index):
        if round_index == 0:
            return None
        return lambda offset: wait_offset(joint_in, s_joint, r_joint, round_index - 1, offset)

    def fit_and_send(turn):
        row = row_at(turn)
        if turn == 0:
            totals = corrupted(row_at_start(joint_apart))
            rests = [noise[pl.ds((place // 2) * 32 + place % 2, TIMES, stride=2), :] + totals[place] for place in range(4)]
        else:
            totals = corrupted(row, wait_joint(turn))
            rests = [observed[place // 2, place % 2] - totals[place] for place in range(4)]
        for offset in (0, 1, 3, 2):
            for slot, (z, which) in enumerate(places):
                patch = z * BL + chip_of(offset) * 2 + which
                for channel in range(2):
                    rest_r, rest_i = rests[2 * channel], rests[2 * channel + 1]
                    mr, mi = model[channel, patch, 0], model[channel, patch, 1]
                    power = energy[patch, channel:channel + 1, :]
                    for part, value in enumerate((mr * rest_r + mi * rest_i, mr * rest_i - mi * rest_r)):
                        at = part * 2 + channel
                        fits[offset][turn, slot, at:at + 1, :] = (
                            jnp.sum(value, axis=0, keepdims=True) + row(offset, slot, at) * power)
            send_offset(fits, fits_in, s_fit, r_fit, turn, offset)

    inverse = None
    weight_halves = None
    weight_rows = None
    for turn in range(ITERS):
        fit_and_send(turn)
        if turn == 0:
            for step in FAR + NEAR[:-1]:
                other = ring(step)[0]
                send_ring(energy.at[other], energy_in.at[me], s_energy, r_energy, other)
            energy_in[me] = energy[me]
            totals = corrupted(row_at_start(joint_true))
            for channel in range(2):
                for part in range(2):
                    observed[channel, part] = noise[pl.ds(channel * 32 + part, TIMES, stride=2), :] + totals[2 * channel + part]
            for source in range(BL):
                for end in range(2):
                    row = ids[source, end:end + 1, :]
                    start = (source * 2 + end) * LANES
                    onehot[:, start:start + LANES] = jnp.where(station == row, 1.0, 0.0).astype(BF16)
            first_copy.wait_recv()
            for channel in range(2):
                own = start_gains[pl.ds(pl.multiple_of(channel * 128 + me * 8, 8), 8), :]
                other = first_in[channel]
                for row in range(8):
                    half, lane, part = row // 4, (row // 2) % 2, row % 2
                    at = half * 4 + part * 2 + channel
                    owned[z_hi, at:at + 1, lane * LANES:(lane + 1) * LANES] = own[row:row + 1]
                    owned[1 - z_hi, at:at + 1, lane * LANES:(lane + 1) * LANES] = other[row:row + 1]
            gains_now = owned[...].reshape(16, 256)
            rows = split_rows(gains_now)
            for chip in range(LINE):
                put_ends(rows, chip)
            for step in NEAR[:-1] + FAR:
                other = ring(step)[0]
                wait_ring(energy_in.at[other], s_energy, r_energy, other)
            weight_rows = jnp.concatenate([energy_in[0, 4:8], energy_in[BL, 4:8]], axis=0)
            weight_rows = jnp.concatenate([weight_rows] * 4, axis=1)
            weight_halves = to_halves(weight_rows)

        received = jnp.zeros((32, STATIONS), F32)
        for offset in (2, 1, 3, 0):
            chip = chip_of(offset)
            wait_offset(fits_in, s_fit, r_fit, turn, offset)
            columns = []
            for which in range(2):
                source = chip * 2 + which
                fit = jnp.concatenate([fits_in[offset][turn, which], fits_in[offset][turn, 2 + which]], axis=0)
                power = jnp.concatenate([energy_in[source, 0:4], energy_in[BL + source, 0:4]], axis=0)
                for toward_first in (True, False):
                    far = (seconds if toward_first else firsts)[source]
                    far_swapped = swapped(far)
                    direct = far * fit
                    crossed = far_swapped * fit
                    if toward_first:
                        numer = jnp.where(is_real, direct - from_later(direct), crossed + from_earlier(crossed))
                    else:
                        numer = jnp.where(is_real, direct + from_later(direct), from_earlier(crossed) - crossed)
                    denom = (far * far + far_swapped * far_swapped) * power
                    columns.append(jnp.concatenate(split_two(jnp.concatenate([numer, denom], axis=0)), axis=0))
            received = received + lax.dot_general(
                jnp.concatenate(columns, axis=1), onehot[:, pl.ds(pl.multiple_of(chip * 512, 512), 512)],
                (((1,), (1,)), ((), ())), preferred_element_type=F32)
        received = received[0:16] + received[16:32]
        solved = (received[0:8] * weight_rows) / jnp.maximum(received[8:16] * weight_rows, 1.0)
        blended = 0.5 * gains_now + 0.5 * to_halves(solved)
        packed = weight_halves * blended

        width = 384 if turn == 0 else 256
        for z in range(2):
            mixed[turn, 2 * x + z, :, 0:256] = packed[z * 8:z * 8 + 8]
            if turn == 0:
                mixed[turn, 2 * x + z, :, 256:384] = weight_halves[z * 8:z * 8 + 8, 0:LANES]

        def planes(first, count):
            return mixed.at[turn, pl.ds(first, count), :, pl.ds(0, width)]

        def far_plane(index):
            return mixed_far.at[turn, pl.ds(index, 1), :, pl.ds(0, width)]

        line_copies, far_copies = [], []
        for other_x in range(LINE):
            up = remote(planes(2 * x + 1, 1), far_plane(x), s_mix.at[turn, 3 + other_x],
                        r_mix.at[turn, 4 + x], plane(y + 1, other_x))
            down = remote(planes(2 * x, 1), far_plane(4 + x), s_mix.at[turn, 7 + other_x],
                          r_mix.at[turn, 8 + x], plane(y - 1, other_x))
            far_copies.append((jnp.logical_and(above, other_x <= x), up))
            far_copies.append((jnp.logical_and(below, other_x >= x), down))
        for needed, copy in far_copies:
            pl.when(needed)(copy.start)
        for step in (2, 1, 3):
            copy = remote(planes(2 * x, 2), planes(2 * x, 2), s_mix.at[turn, step - 1], r_mix.at[turn, x],
                          plane(y, lax.rem(x + step, LINE)))
            copy.start()
            line_copies.append(copy)

        for step in range(1, LINE):
            source_x = lax.rem(x + step, LINE)
            remote(planes(2 * source_x, 2), planes(2 * source_x, 2), s_mix.at[turn, step - 1],
                   r_mix.at[turn, source_x], plane(y, source_x)).wait_recv()

        def smoothed(planes_now, first):
            high, low = split_two(planes_now[turn, :, :, 0:width].reshape(64, width))
            both = jnp.dot(smoothing_both[:, first:first + 64], high, preferred_element_type=F32)
            return both[0:16] + both[16:32] + jnp.dot(smoothing_high[:, first:first + 64], low, preferred_element_type=F32)

        summed = smoothed(mixed, 0)
        for source_x in range(LINE):
            from_above = remote(far_plane(4 + source_x), far_plane(4 + source_x), s_mix.at[turn, 3 + source_x],
                                r_mix.at[turn, 8 + source_x], plane(y + 1, source_x))
            from_below = remote(far_plane(source_x), far_plane(source_x), s_mix.at[turn, 7 + source_x],
                                r_mix.at[turn, 4 + source_x], plane(y - 1, source_x))
            pl.when(jnp.logical_and(above, source_x <= x))(from_above.wait_recv)
            pl.when(jnp.logical_and(below, source_x >= x))(from_below.wait_recv)
        summed = summed + smoothed(mixed_far, 64)
        if turn == 0:
            inverse = 1.0 / jnp.maximum(summed[:, 256:384], 1.0)
            inverse = jnp.concatenate([inverse, inverse], axis=1)
        gains_now = summed[:, 0:256] * inverse

        earlier = len(sends)
        if turn == ITERS - 1:
            for z in range(2):
                for channel in range(2):
                    for row in range(8):
                        half, lane, part = row // 4, (row // 2) % 2, row % 2
                        at = z * 8 + half * 4 + part * 2 + channel
                        stage[z, channel, row:row + 1, :] = gains_now[at:at + 1, lane * LANES:(lane + 1) * LANES]
            for step in FAR + NEAR[:-1]:
                other = ring(step)[0]
                send_ring(stage.at[lax.div(other, BL)], gains_out.at[:, me], s_gain, r_gain, other)
            gains_out[:, me] = stage[z_hi]

        rows = split_rows(gains_now)
        for offset in (0, 1, 3, 2):
            chip = chip_of(offset)
            for which, (near, far) in enumerate(put_ends(rows, chip)):
                direct = near * far
                crossed = near * swapped(far)
                joint = jnp.where(is_real, direct + from_later(direct), crossed - from_earlier(crossed))
                joint_out[offset][turn, which] = joint[0:4]
                joint_out[offset][turn, 2 + which] = joint[4:8]
            send_offset(joint_out, joint_in, s_joint, r_joint, turn, offset)
        if turn == ITERS - 1:
            for copy in sends[:earlier]:
                copy.wait_send()

        for copy in line_copies:
            copy.wait_send()
        for needed, copy in far_copies:
            pl.when(needed)(copy.wait_send)

    totals = corrupted(row_at(ITERS), wait_joint(ITERS))
    for channel in range(2):
        for part in range(2):
            residual_out[pl.ds(channel * 32 + part, TIMES, stride=2), :] = (
                observed[channel, part] - totals[2 * channel + part])
    for step in NEAR[:-1] + FAR:
        other = ring(step)[0]
        wait_ring(gains_out.at[:, other], s_gain, r_gain, other)
    for copy in sends[earlier:]:
        copy.wait_send()


def local(visibility_noise, baseline_wavelength_coords, station_pair, comp_position, comp_flux,
          comp_spectral, comp_count, true_gains, start_gains, channel_flags):
    vmem = pl.BlockSpec(memory_space=VMEM)
    smem = pl.BlockSpec(memory_space=SMEM)
    anywhere = pl.BlockSpec(memory_space=pltpu.MemorySpace.HBM)
    dma = pltpu.SemaphoreType.DMA
    def tiles(gains):
        return gains.reshape(2, DIRS, 2, 4, LANES).transpose(0, 1, 3, 2, 4).reshape(2 * DIRS * 8, LANES)

    gains, residual = pl.pallas_call(
        calibrate_kernel,
        out_shape=(pltpu.VMEM((2, DIRS, 8, LANES), F32), pltpu.VMEM((64, LANES), F32)),
        in_specs=[anywhere, anywhere, vmem, vmem, vmem, vmem, smem, anywhere, anywhere, smem],
        out_specs=(vmem, vmem),
        scratch_shapes=[
            pltpu.VMEM((64, LANES), F32),
            pltpu.VMEM((3, TIMES, LANES), F32),
            pltpu.VMEM((256, LANES), F32),
            pltpu.VMEM((256, LANES), F32),
            pltpu.VMEM((BL, 8, LANES), F32),
            pltpu.VMEM((BL, 8, LANES), jnp.int32),
            pltpu.VMEM((BL, LANES), jnp.int32),
            pltpu.SMEM((BL, 8, LANES), F32),
            pltpu.SMEM((BL, LANES), jnp.int32),
            pltpu.VMEM((COMPONENTS, 4, TIMES, LANES), F32),
            pltpu.VMEM((2, DIRS, 2, TIMES, LANES), F32),
            pltpu.VMEM((STATIONS, 2 * LANES), BF16),
            pltpu.VMEM((STATIONS, BL * 2 * LANES), BF16),
            pltpu.VMEM((2, 2, TIMES, LANES), F32),
            pltpu.VMEM((LINE, 4, 4, LANES), F32),
            pltpu.VMEM((BL, 8, LANES), F32),
            pltpu.VMEM((BL, 8, LANES), F32),
            pltpu.VMEM((2, 8, 256), F32),
            pltpu.VMEM((2, 8, LANES), F32),
            pltpu.VMEM((2, 8, LANES), F32),
            pltpu.VMEM((RING, 8, LANES), F32),
            pltpu.VMEM((RING, 8, LANES), F32),
            pltpu.VMEM((LINE, 4, 4, LANES), F32),
            pltpu.VMEM((LINE, 4, 4, LANES), F32),
        ] + [pltpu.VMEM((ITERS, 4, 4, LANES), F32)] * 16 + [
            pltpu.VMEM((ITERS, 8, 8, 384), F32),
            pltpu.VMEM((ITERS, 8, 8, 384), F32),
            pltpu.VMEM((2, 2, 8, LANES), F32),
            dma((6,)), dma((BL,)), dma((BL,)), dma((BL,)), dma((BL,)),
            dma(()), dma(()),
            dma((RING,)), dma((RING,)),
            dma((ITERS, RING)), dma((ITERS, RING)),
            dma((ITERS, RING)), dma((ITERS, RING)),
            dma((ITERS, 11)), dma((ITERS, 12)),
            dma((RING,)), dma((RING,)),
        ],
        compiler_params=pltpu.CompilerParams(
            collective_id=0, has_side_effects=True, vmem_limit_bytes=56 * 1024 * 1024),
        name="calibrate",
    )(visibility_noise.reshape(64, LANES), baseline_wavelength_coords, station_pair, comp_position, comp_flux,
      comp_spectral, comp_count, tiles(true_gains), tiles(start_gains), channel_flags)
    gains = gains.reshape(2, DIRS, 4, 2, LANES).transpose(0, 1, 3, 2, 4).reshape(2, DIRS, 2, STATIONS)
    return gains, residual.reshape(2, TIMES, 2, LANES)


def solution(mesh):
    in_specs = (
        P("freq", None, None, "bl"),
        P(None, None, "bl"),
        P(None, "bl"),
        P("bl", None, None),
        P("bl", None),
        P("bl", None),
        P("bl"),
        P("freq", None, None, None),
        P("freq", None, None, None),
        P("freq"),
    )
    out_specs = (P("freq", None, None, None), P("freq", None, None, "bl"))
    return jax.shard_map(local, mesh=mesh, in_specs=in_specs, out_specs=out_specs, check_vma=False)
```
